256 devices in a mesh: gz: 64 (over y_hi, x, z), gy: 4 (over y_lo, core).
Axes of the slice: x: 4, y: 4 (y_hi: 2, y_lo: 2; y = y_hi * 2 + y_lo), z: 8, core: 2. Of those that a mesh axis runs over, the one named last changes fastest.
Arguments:
- concentration: float32 [1024, 128, 128], P('gz', 'gy'), may hold values from -0.9 to 0.9
- cotangent: float32 [1024, 128, 128], P('gz', 'gy'), may hold values from -12 to 12
- w_in: float32 [32, 4], replicated, may hold values from -3 to 3
- b_in: float32 [32], replicated, may hold values from -1 to 1
- w_out: float32 [32], replicated, may hold values from -1 to 1
- b_out: float32 [], replicated, may hold values from -1 to 1
Outputs:
- grad_concentration: float32 [1024, 128, 128], P('gz', 'gy')
- grad_w_in: float32 [32, 4], replicated
- grad_b_in: float32 [32], replicated
- grad_w_out: float32 [32], replicated
- grad_b_out: float32 [], replicated
The draws below stay inside these ranges and needn't reach their ends.
All inputs are finite; a program needn't handle non-finite values.
Results may differ from the reference program's by a relative error of at most 0.00055.
Values sent between devices are 32-bit elements; how exact they have to be, the bound alone decides.
A program may use at most 64 MiB of HBM per device.

```python
import math
import jax
import jax.numpy as jnp
from jax import lax

UNITS = 32
INPUTS = 4
NX = 128
NY = 128
NZ = 1024


def draw_cotangent(key, part):
    key = jax.random.fold_in(key, 11)
    depth = (jnp.arange(NZ, dtype=jnp.float32) / NZ)[:, None, None]
    noise = jnp.clip(jax.random.normal(key, (NZ, NY, NX), jnp.float32), -4.0, 4.0)
    return noise * (1.0 + 2.0 * depth)


def steps_of(stream_key, shape, shards, low, high):
    def one(axis_at, blocks):
        draws = jax.random.uniform(jax.random.fold_in(jax.random.fold_in(stream_key, 6), axis_at), (blocks,), jnp.float32, low / len(shards), high / len(shards))
        return jnp.repeat(jnp.exp(draws), shape[axis_at] // blocks).reshape((-1,) + (1,) * (len(shape) - axis_at - 1))

    factor_of = one(*shards[0])
    for cut in shards[1:]:
        factor_of = factor_of * one(*cut)
    return factor_of


def gaussian(key, shape, deviation, bound, kind=jnp.bfloat16):
    return jnp.clip(deviation * jax.random.normal(key, shape, jnp.float32), -bound, bound).astype(kind)


def setup_inputs(seed: int = 0) -> dict:
    key_list = jax.random.split(jax.random.key(seed), 7)
    return {
        "concentration": jnp.clip(jax.random.uniform(key_list[0], (NZ, NY, NX), jnp.float32, -0.9, 0.9) * steps_of(key_list[0], (NZ, NY, NX), ((0, 64), (1, 4)), -0.4, 0.0), -0.9, 0.9),
        "cotangent": draw_cotangent(jax.random.fold_in(key_list[6], 71), 0),
        "w_in": gaussian(key_list[2], (UNITS, INPUTS), INPUTS ** -0.5, 3.0, jnp.float32),
        "b_in": jnp.clip(jax.random.uniform(key_list[3], (UNITS,), jnp.float32, -1.0, 1.0), -1.0, 1.0),
        "w_out": gaussian(key_list[4], (UNITS,), UNITS ** -0.5, 1.0, jnp.float32),
        "b_out": jnp.clip(jax.random.uniform(key_list[5], (), jnp.float32, -1.0, 1.0), -1.0, 1.0),
    }


KAPPA = 0.5
STEP = 0.008
FLOOR = 0.05
HIGH = lax.Precision.HIGHEST

def neighbours(padded):
    centre = padded[1:-1, 1:-1]
    return (centre, [padded[2:, 1:-1], padded[:-2, 1:-1], padded[1:-1, 2:], padded[1:-1, :-2], jnp.roll(centre, -1, 2), jnp.roll(centre, 1, 2)])

def local_fields(padded):
    cells, near = neighbours(padded)
    laplace = sum(near) - 6.0 * cells
    slopes = [0.5 * (near[0] - near[1]), 0.5 * (near[2] - near[3]), 0.5 * (near[4] - near[5])]
    square = slopes[0] * slopes[0] + slopes[1] * slopes[1] + slopes[2] * slopes[2]
    potential = cells * cells * cells - cells - KAPPA * laplace
    features = jnp.stack([cells, laplace, square, potential], axis=1)
    return (cells, features)

def plane_mobility(params, plane):
    w_in, b_in, w_out, b_out = params
    pre = jnp.einsum('jk,kyx->jyx', w_in, plane, precision=HIGH) + b_in[:, None, None]
    score = jnp.einsum('j,jyx->yx', w_out, jnp.tanh(pre), precision=HIGH) + b_out
    return jax.nn.softplus(score) + FLOOR

def flux_sum(pot_pad, mob_pad):
    centre_pot, near_pot = neighbours(pot_pad)
    centre_mob, near_mob = neighbours(mob_pad)
    total = jnp.zeros_like(centre_pot)
    for other_pot, other_mob in zip(near_pot, near_mob):
        total = total + 0.5 * (other_mob + centre_mob) * (other_pot - centre_pot)
    return total

def wrapped(field):
    return jnp.pad(field, ((1, 1), (1, 1), (0, 0)), mode='wrap')

def one_step(conc, params):
    cells, features = local_fields(wrapped(conc))
    mobile = lax.map(jax.checkpoint(lambda plane: plane_mobility(params, plane)), features)
    return cells + STEP * flux_sum(wrapped(features[:, 3]), wrapped(mobile))

def reference(concentration, cotangent, w_in, b_in, w_out, b_out):

    def run(conc, wi, bi, wo, bo):
        params = (wi, bi, wo, bo)
        return one_step(one_step(conc, params), params)
    result, pull = jax.vjp(run, concentration, w_in, b_in, w_out, b_out)
    grads = pull(cotangent)
    factor = 1.0 / (STEP * math.sqrt(float(NX * NY * NZ)))
    return (grads[0], grads[1] * factor, grads[2] * factor, grads[3] * factor, grads[4] * factor)
```

```python
import math

import jax
import jax.numpy as jnp
from jax import lax
from jax.experimental import pallas as pl
from jax.experimental.pallas import tpu as pltpu
from jax.sharding import PartitionSpec as P

KAPPA = 0.5
STEP = 0.008
FLOOR = 0.05
HIGH = lax.Precision.HIGHEST
MESH = pl.DeviceIdType.MESH
F32 = jnp.float32
BF16 = jnp.bfloat16

WC = 7
WA = 4
R = 8
UNITS = 32
ROWS = UNITS * 8


DIRECTIONS = [(dz, dy) for dz in (0, -1, 1) for dy in (-1, 1, 0) if (dz, dy) != (0, 0)]


def iota(shape, dim):
    return lax.broadcasted_iota(jnp.int32, shape, dim)


def xp(v):
    return pltpu.roll(v, v.shape[1] - 1, 1)


def xm(v):
    return pltpu.roll(v, 1, 1)


def yp(v):
    return pltpu.roll(v, v.shape[0] - 1, 0)


def ym(v):
    return pltpu.roll(v, 1, 0)


def split(v):
    high = v.astype(BF16)
    return high, (v - high.astype(F32)).astype(BF16)


def dot(a, b, precision=None):
    return jnp.dot(a, b, preferred_element_type=F32, precision=precision)


def make_kernel(zl, yl, ng, ny, factor):
    nv = yl // 8
    yr = yl + 2 * R
    g1 = 4 if ng % 4 == 0 else 1
    size1 = g1 * ny
    size2 = ng // g1

    def kernel(
        conc, cot, w_in, b_in, w_out, b_out,
        out, out_wi, out_bi, out_wo, out_bo,
        C, A0, MU1, M1, SG1, C2, MU2, M2, SG2, RR, UU, VV, A1, H1, H2,
        WL, WOF, CT, UB, PACC, TACC, GACC, OUTV, RED, RED2, MSG, MSG2,
        send_sem, recv_sem, local_sem, rs_send, rs_recv, rs2_send, rs2_recv,
    ):
        gz = lax.axis_index("gz")
        gy = lax.axis_index("gy")

        def neighbour(dz, dy):
            return (lax.rem(gz + dz + ng, ng), lax.rem(gy + dy + ny, ny))

        block1 = gz // g1
        place1 = lax.rem(gz, g1) * ny + gy
        place2 = block1

        def peer1(k):
            q = lax.rem(place1 + k, size1)
            return q, (block1 * g1 + q // ny, lax.rem(q, ny))

        def peer2(k):
            q = lax.rem(place2 + k, size2)
            return q, (q * g1 + lax.rem(gz, g1), gy)

        local_c = pltpu.make_async_copy(
            conc, C.at[pl.ds(WC, zl), pl.ds(R, yl)], local_sem.at[0])
        local_a = pltpu.make_async_copy(
            cot, A0.at[pl.ds(WA, zl), pl.ds(R, yl)], local_sem.at[1])
        local_c.start()
        local_a.start()

        barrier = pltpu.get_barrier_semaphore()
        count = 0
        for dz, dy in DIRECTIONS:
            pl.semaphore_signal(barrier, inc=1, device_id=neighbour(dz, dy), device_id_type=MESH)
            count += 1
        for k in range(1, size1):
            pl.semaphore_signal(barrier, inc=1, device_id=peer1(k)[1], device_id_type=MESH)
            count += 1
        for k in range(1, size2):
            pl.semaphore_signal(barrier, inc=1, device_id=peer2(k)[1], device_id_type=MESH)
            count += 1
        pl.semaphore_wait(barrier, count)

        def span_z(dz, width):
            if dz > 0:
                return pl.ds(zl - width, width), pl.ds(0, width)
            if dz < 0:
                return pl.ds(0, width), pl.ds(width + zl, width)
            return pl.ds(0, zl), pl.ds(width, zl)

        def span_y(dy):
            if dy > 0:
                return pl.ds(yl - R, R), pl.ds(0, R)
            if dy < 0:
                return pl.ds(0, R), pl.ds(R + yl, R)
            return pl.ds(0, yl), pl.ds(R, yl)

        def halo(which, source, field, width):
            copies = []
            for n, (dz, dy) in enumerate(DIRECTIONS):
                sz, tz = span_z(dz, width)
                sy, ty = span_y(dy)
                copies.append(pltpu.make_async_remote_copy(
                    src_ref=source.at[sz, sy],
                    dst_ref=field.at[tz, ty],
                    send_sem=send_sem.at[which, n],
                    recv_sem=recv_sem.at[which, n],
                    device_id=neighbour(dz, dy),
                    device_id_type=MESH,
                ))
            return copies

        halo_c = halo(0, conc, C, WC)
        halo_a = halo(1, cot, A0, WA)
        for copy in halo_c:
            copy.start()
        for copy in halo_a:
            copy.start()

        lane = iota((UNITS, 128), 1)
        eye = iota((UNITS, UNITS), 0) == iota((UNITS, UNITS), 1)
        bi_col = jnp.sum(jnp.where(eye, b_in[...], 0.0), axis=1, keepdims=True)
        wo_col = jnp.sum(jnp.where(eye, w_out[...], 0.0), axis=1, keepdims=True)
        packed = jnp.where(lane == 4, bi_col, jnp.where(lane == 5, wo_col, 0.0))
        for k in range(4):
            packed = jnp.where(lane == k, w_in[:, k:k + 1], packed)
        spread = (iota((ROWS, UNITS), 0) // 8 == iota((ROWS, UNITS), 1)).astype(F32)
        params = dot(spread, packed, HIGH)
        row = iota((ROWS, 128), 0)
        col = iota((ROWS, 128), 1)
        same = (row & 7) == (col & 7)
        which_k = (col & 31) // 8
        group = col // 32
        w_sel = jnp.zeros((ROWS, 128), F32)
        for k in range(4):
            w_sel = jnp.where(which_k == k, params[:, k:k + 1], w_sel)
        bias = jnp.broadcast_to(params[:, 4:5], (ROWS, 128))
        wo_full = jnp.broadcast_to(params[:, 5:6], (ROWS, 128))
        WOF[...] = wo_full
        value = jnp.where(group == 3, jnp.where(which_k < 2, bias, 0.0), w_sel)
        high = value.astype(BF16).astype(F32)
        low = value - high
        is_low = (group == 1) | ((group == 3) & (which_k == 1))
        WL[...] = jnp.where(same, jnp.where(is_low, low, high), 0.0).astype(BF16)
        joint = w_sel * wo_full
        j_high = joint.astype(BF16).astype(F32)
        j_low = joint - j_high
        j_mat = jnp.where(same, jnp.where(group == 0, j_high, jnp.where(group == 1, j_low, 0.0)), 0.0)
        CT[...] = j_mat.T[0:64].astype(BF16)
        PACC[...] = jnp.zeros((2 * ROWS, 128), F32)
        TACC[...] = jnp.zeros((ROWS, 128), F32)
        GACC[...] = jnp.zeros((8, 128), F32)

        half = iota((8, 128), 0) < 4

        def pack(v):
            blocks = [v[R + 8 * i:R + 8 * i + 8] for i in range(nv)]
            blocks.append(jnp.where(half, v[R + yl:], v[:R]))
            return blocks

        def unpack(blocks):
            return jnp.concatenate([blocks[-1]] + blocks[:-1] + [blocks[-1]], axis=0)

        def fields_of(c_ref, p):
            c = c_ref[p]
            zu, zd = c_ref[p + 1], c_ref[p - 1]
            yu, yd = yp(c), ym(c)
            xu, xd = xp(c), xm(c)
            lap = ((zu + zd) + (yu + yd)) + (xu + xd) - 6.0 * c
            s0, s1, s2 = 0.5 * (zu - zd), 0.5 * (yu - yd), 0.5 * (xu - xd)
            sq = s0 * s0 + s1 * s1 + s2 * s2
            return c, lap, sq, (s0, s1, s2)

        def units(pair):
            feats = jnp.concatenate([jnp.concatenate(f, axis=0) for f in pair], axis=1)
            f_high, f_low = split(feats)
            rhs = jnp.concatenate([f_high, f_high, f_low, jnp.ones((32, 256), BF16)], axis=0)
            return jnp.tanh(dot(WL[...], rhs))

        def score(h):
            wo = WOF[...]
            weighted = h * jnp.concatenate([wo, wo], axis=1)
            return jnp.sum(weighted.reshape(UNITS, 8, 256), axis=0) + b_out[0, 0]

        def soft(s):
            e = jnp.exp(s)
            return jnp.log(1.0 + e) + FLOOR, e / (1.0 + e)

        def forward_one(p):
            for d in range(2):
                q = p + d
                c, lap, sq, _ = fields_of(C, q)
                mu = c * c * c - c - KAPPA * lap
                MU1[q] = mu
                feats = [c, lap, sq, mu]
                for a in range(0, nv + 2, 2):
                    ids = [1 + a, 2 + a] if a < nv else [nv + 1, 0]
                    pair = [[f[8 * i:8 * i + 8] for f in feats] for i in ids]
                    h = units(pair)
                    if a < nv:
                        H1[q, a] = h[:, :128]
                        H1[q, a + 1] = h[:, 128:]
                    else:
                        mask = (iota((ROWS, 128), 0) & 7) < 4
                        H1[q, nv] = jnp.where(mask, h[:, :128], h[:, 128:])
                    m, sg = soft(score(h))
                    for i in range(2):
                        rows = pl.ds(8 * ids[i], 8)
                        M1[q, rows] = m[:, 128 * i:128 * i + 128]
                        SG1[q, rows] = sg[:, 128 * i:128 * i + 128]

        def loop(first, last, body, step=2):
            def run(i, carry):
                body(first + step * i)
                return carry
            lax.fori_loop(0, (last - first) // step, run, 0)

        local_c.wait()
        for n in range(2):
            halo_c[n].wait_recv()
        loop(WC + 2, WC + zl - 2, forward_one)
        for n in range(2, 8):
            halo_c[n].wait_recv()
        loop(1, WC + 2, forward_one)
        loop(WC + zl - 2, 2 * WC + zl - 1, forward_one)

        def advance(p):
            mu, m = MU1[p], M1[p]
            def face(mu_a, m_a, mu_b, m_b):
                return (m_a + m_b) * (mu_b - mu_a)
            up = face(mu, m, MU1[p + 1], M1[p + 1])
            down = face(MU1[p - 1], M1[p - 1], mu, m)
            fy = face(mu, m, yp(mu), yp(m))
            fx = face(mu, m, xp(mu), xp(m))
            total = (up - down) + (fy - ym(fy)) + (fx - xm(fx))
            C2[p] = C[p] + (0.5 * STEP) * total

        loop(2, 2 * WC + zl - 2, advance, 1)

        def forward_two(p):
            feats = []
            for d in range(2):
                q = p + d
                c, lap, sq, _ = fields_of(C2, q)
                mu = c * c * c - c - KAPPA * lap
                MU2[q] = mu
                feats.append([pack(f) for f in (c, lap, sq, mu)])
            work = [((d, a), (d, a + 1)) for d in range(2) for a in range(0, nv, 2)] + [((0, nv), (1, nv))]
            for places in work:
                h = units([[f[a] for f in feats[d]] for d, a in places])
                m, sg = soft(score(h))
                for i, (d, a) in enumerate(places):
                    q = p + d
                    H2[q, a] = h[:, 128 * i:128 * i + 128]
                    mi, si = m[:, 128 * i:128 * i + 128], sg[:, 128 * i:128 * i + 128]
                    for start in ([R + 8 * a] if a < nv else [0, R + yl]):
                        M2[q, pl.ds(start, 8)] = mi
                        SG2[q, pl.ds(start, 8)] = si

        loop(3, 2 * WC + zl - 3, forward_two)

        def backward(p, adj, shift, c_ref, mu_ref, m_ref, sg_ref, h_ref):
            states = []
            for q in p:
                c, lap, sq, slopes = fields_of(c_ref, q)
                mu, m, a = mu_ref[q], m_ref[q], adj[q + shift]
                def faces(mu_a, m_a, a_a, mu_b, m_b, a_b):
                    da = a_b - a_a
                    return (mu_b - mu_a) * da, (m_a + m_b) * da
                q_up, r_up = faces(mu, m, a, mu_ref[q + 1], m_ref[q + 1], adj[q + 1 + shift])
                q_dn, r_dn = faces(mu_ref[q - 1], m_ref[q - 1], adj[q - 1 + shift], mu, m, a)
                q_y, r_y = faces(mu, m, a, yp(mu), yp(m), yp(a))
                q_x, r_x = faces(mu, m, a, xp(mu), xp(m), xp(a))
                adj_mob = (q_up + q_dn) + (q_y + ym(q_y)) + (q_x + xm(q_x))
                adj_pot = (r_up - r_dn) + (r_y - ym(r_y)) + (r_x - xm(r_x))
                g = (-0.5 * STEP) * adj_mob * sg_ref[q]
                adj_pot = (0.5 * STEP) * adj_pot
                states.append(dict(c=c, a=a, slopes=slopes, adj_pot=adj_pot, g=pack(g), f=[pack(f) for f in (c, lap, sq, mu)], A={}))

            work = [((d, b), (d, b + 1)) for d in range(2) for b in range(0, nv, 2)] + [((0, nv), (1, nv))]
            gg = []
            for n, places in enumerate(work):
                h = jnp.concatenate([h_ref[p[d], b] for d, b in places], axis=1)
                u = 1.0 - h * h
                u_high = u.astype(BF16)
                back = dot(CT[...], u_high)
                back = back[:32] + back[32:]
                g = jnp.concatenate([states[d]["g"][b] for d, b in places], axis=1)
                for i, (d, b) in enumerate(places):
                    states[d]["A"][b] = [
                        back[8 * k:8 * k + 8, 128 * i:128 * i + 128] * states[d]["g"][b] for k in range(4)
                    ]
                if n < len(work) - 1:
                    UB[pl.ds(0, ROWS), pl.ds(256 * n, 256)] = u_high
                    UB[pl.ds(ROWS, ROWS), pl.ds(256 * n, 256)] = (u - u_high.astype(F32)).astype(BF16)
                    feats = [jnp.concatenate([states[d]["f"][k][b] for d, b in places], axis=1) for k in range(4)]
                    stack = jnp.concatenate([g * f for f in feats] + [g, jnp.zeros((8, 256), F32)], axis=0)
                    s_high, s_low = split(stack)
                    gg.append(jnp.concatenate([s_high, s_low, jnp.zeros((32, 256), BF16)], axis=0))
            return states, gg

        def sums(p, states, gg, h_ref):
            rhs = jnp.concatenate(gg, axis=1)
            PACC[...] += lax.dot_general(
                UB[...], rhs, (((1,), (1,)), ((), ())), preferred_element_type=F32)
            total = TACC[...].reshape(UNITS, 8, 128)
            g_total = GACC[...]
            for d in range(2):
                for b in range(nv):
                    g = states[d]["g"][b]
                    total = total + h_ref[p[d], b].reshape(UNITS, 8, 128) * g[None]
                    g_total = g_total + g
            TACC[...] = total.reshape(ROWS, 128)
            GACC[...] = g_total

        def finish(p, states):
            for d in range(2):
                s = states[d]
                A = [unpack([s["A"][b][k] for b in range(nv + 1)]) for k in range(4)]
                adj_pot = s["adj_pot"] + A[3]
                adj_lap = A[1] - KAPPA * adj_pot
                zed, why, ex = (A[2] * slope for slope in s["slopes"])
                rest = s["a"] + A[0] + (3.0 * s["c"] * s["c"] - 1.0) * adj_pot - 6.0 * adj_lap
                rest = rest + (xm(adj_lap + ex) + xp(adj_lap - ex)) + (ym(adj_lap + why) + yp(adj_lap - why))
                RR[p[d]] = rest
                UU[p[d]] = adj_lap + zed
                VV[p[d]] = adj_lap - zed

        for copy in halo_a:
            copy.wait_recv()
        local_a.wait()

        def back_two(with_sums):
            def body(p):
                states, gg = backward(p, A0, WA - WC, C2, MU2, M2, SG2, H2)
                if with_sums:
                    sums(p, states, gg, H2)
                finish(p, states)
            return body

        def back_one(with_sums):
            def body(p):
                states, gg = backward(p, A1, 0, C, MU1, M1, SG1, H1)
                if with_sums:
                    sums(p, states, gg, H1)
                finish(p, states)
            return body

        loop(0, 3, lambda k: back_two(False)((WC - 1 - k, WC + zl + k)), 1)
        loop(WC, WC + zl, lambda p: back_two(True)((p, p + 1)))

        def join(p):
            A1[p] = RR[p] + UU[p - 1] + VV[p + 1]

        loop(WC - 2, WC + zl + 2, join, 1)

        loop(WC, WC + zl, lambda p: back_one(True)((p, p + 1)))
        back_one(False)((WC - 1, WC + zl))

        both = PACC[pl.ds(0, ROWS)] + PACC[pl.ds(ROWS, ROWS)]
        both = jnp.where(same & (col < 96), both, 0.0)
        gather = (iota((UNITS, ROWS), 1) // 8 == iota((UNITS, ROWS), 0)).astype(F32)
        by_unit = dot(gather, both, HIGH)
        c_row = iota((128, 128), 0)
        c_col = iota((128, 128), 1)
        c_k = jnp.where(c_row < 48, c_row, c_row - 48) // 8
        collect = ((c_k == c_col) & (c_row < 96) & (c_col < 5)).astype(F32)
        grads = dot(by_unit, collect, HIGH) * wo_col
        t_col = jnp.sum(dot(gather, TACC[...], HIGH), axis=1, keepdims=True)
        g_sum = jnp.sum(jnp.sum(GACC[...], axis=0, keepdims=True), axis=1, keepdims=True)
        first_row = iota((UNITS, 128), 0) == 0
        grads = jnp.where(lane == 5, t_col, grads)
        grads = jnp.where((lane == 6) & first_row, g_sum, grads)
        message = grads[0:8]
        for n in range(1, 4):
            message = message + pltpu.roll(grads[8 * n:8 * n + 8], 32 * n, 1)
        MSG[...] = message

        def exchange(size, place, peer, src, slots, s_sem, r_sem):
            copies = []
            for k in range(1, size):
                q, device = peer(k)
                copy = pltpu.make_async_remote_copy(
                    src_ref=src, dst_ref=slots.at[place], send_sem=s_sem.at[k],
                    recv_sem=r_sem.at[place], device_id=device, device_id_type=MESH)
                copy.start()
                copies.append(copy)
            slots[place] = src[...]
            return copies

        def collected(size, peer, copies, src, slots, s_sem, r_sem):
            for k in range(1, size):
                q, device = peer(k)
                pltpu.make_async_remote_copy(
                    src_ref=src, dst_ref=slots.at[q], send_sem=s_sem.at[k],
                    recv_sem=r_sem.at[q], device_id=device, device_id_type=MESH).wait_recv()
            total = slots[0]
            for k in range(1, size):
                total = total + slots[k]
            return total

        sent1 = exchange(size1, place1, peer1, MSG, RED, rs_send, rs_recv)

        def result(p):
            rows = pl.ds(R, yl)
            OUTV[p - WC] = RR[p, rows] + UU[p - 1, rows] + VV[p + 1, rows]

        loop(WC, WC + zl, result, 1)
        write = pltpu.make_async_copy(OUTV, out, local_sem.at[2])
        write.start()

        total = collected(size1, peer1, sent1, MSG, RED, rs_send, rs_recv)
        MSG2[...] = total
        if size2 > 1:
            sent2 = exchange(size2, place2, peer2, MSG2, RED2, rs2_send, rs2_recv)
            total = collected(size2, peer2, sent2, MSG2, RED2, rs2_send, rs2_recv)
        else:
            sent2 = []
        total = total * factor
        full = jnp.concatenate([total] + [pltpu.roll(total, 128 - 32 * n, 1) for n in range(1, 4)], axis=0)
        out_wi[...] = full[:, 0:4]
        out_bi[...] = jnp.sum(jnp.where(eye, full[:, 4:5], 0.0), axis=0, keepdims=True)
        out_wo[...] = jnp.sum(jnp.where(eye, full[:, 5:6], 0.0), axis=0, keepdims=True)
        out_bo[...] = full[0:1, 6:7]

        for copy in halo_c + halo_a + sent1 + sent2:
            copy.wait_send()
        write.wait()

    return kernel, yr, size1, size2


def per_device(ng, ny, concentration, cotangent, w_in, b_in, w_out, b_out):
    zl, yl, nx = concentration.shape
    factor = 1.0 / (STEP * math.sqrt(float(zl * yl * nx * ng * ny)))
    kernel, yr, size1, size2 = make_kernel(zl, yl, ng, ny, factor)
    planes = zl + 2 * WC
    nv = yl // 8
    field = pltpu.VMEM((planes, yr, nx), F32)
    anywhere = pl.BlockSpec(memory_space=pl.ANY)
    vmem = pl.BlockSpec(memory_space=pltpu.VMEM)
    smem = pl.BlockSpec(memory_space=pltpu.SMEM)
    outs = pl.pallas_call(
        kernel,
        out_shape=(
            jax.ShapeDtypeStruct(concentration.shape, F32),
            jax.ShapeDtypeStruct((UNITS, 4), F32),
            jax.ShapeDtypeStruct((1, UNITS), F32),
            jax.ShapeDtypeStruct((1, UNITS), F32),
            jax.ShapeDtypeStruct((1, 1), F32),
        ),
        in_specs=[anywhere, anywhere, vmem, vmem, vmem, smem],
        out_specs=(anywhere, vmem, vmem, vmem, vmem),
        scratch_shapes=[
            field,
            pltpu.VMEM((zl + 2 * WA, yr, nx), F32),
            field, field, field,
            field, field, field, field,
            field, field, field, field,
            pltpu.VMEM((planes, nv + 1, ROWS, nx), F32),
            pltpu.VMEM((planes, nv + 1, ROWS, nx), F32),
            pltpu.VMEM((ROWS, 128), BF16),
            pltpu.VMEM((ROWS, 128), F32),
            pltpu.VMEM((64, ROWS), BF16),
            pltpu.VMEM((2 * ROWS, 2 * yl // 8 * 128), BF16),
            pltpu.VMEM((2 * ROWS, 128), F32),
            pltpu.VMEM((ROWS, 128), F32),
            pltpu.VMEM((8, 128), F32),
            pltpu.VMEM((zl, yl, nx), F32),
            pltpu.VMEM((size1, 8, 128), F32),
            pltpu.VMEM((max(size2, 1), 8, 128), F32),
            pltpu.VMEM((8, 128), F32),
            pltpu.VMEM((8, 128), F32),
            pltpu.SemaphoreType.DMA((2, 8)),
            pltpu.SemaphoreType.DMA((2, 8)),
            pltpu.SemaphoreType.DMA((3,)),
            pltpu.SemaphoreType.DMA((size1,)),
            pltpu.SemaphoreType.DMA((size1,)),
            pltpu.SemaphoreType.DMA((size2,)),
            pltpu.SemaphoreType.DMA((size2,)),
        ],
        compiler_params=pltpu.CompilerParams(
            collective_id=0, has_side_effects=True, vmem_limit_bytes=60 * 1024 * 1024
        ),
    )(
        concentration, cotangent, w_in, b_in.reshape(1, UNITS), w_out.reshape(1, UNITS), b_out.reshape(1, 1)
    )
    return (outs[0], outs[1], outs[2].reshape(UNITS), outs[3].reshape(UNITS), outs[4].reshape(()))


def solution(mesh):
    ng, ny = mesh.shape["gz"], mesh.shape["gy"]
    in_specs = (P("gz", "gy", None), P("gz", "gy", None), P(), P(), P(), P())
    out_specs = (P("gz", "gy", None), P(), P(), P(), P())

    def run(*args):
        return per_device(ng, ny, *args)

    return jax.shard_map(run, mesh=mesh, in_specs=in_specs, out_specs=out_specs, check_vma=False)
```

```python
import math

import jax
import jax.numpy as jnp
from jax import lax
from jax.experimental import pallas as pl
from jax.experimental.pallas import tpu as pltpu
from jax.sharding import PartitionSpec as P

KAPPA = 0.5
STEP = 0.008
FLOOR = 0.05
HIGH = lax.Precision.HIGHEST
MESH = pl.DeviceIdType.MESH
F32 = jnp.float32
BF16 = jnp.bfloat16

WC = 7
WA = 4
R = 8
UNITS = 32
ROWS = UNITS * 8


DIRECTIONS = [(dz, dy) for dz in (0, -1, 1) for dy in (-1, 1, 0) if (dz, dy) != (0, 0)]


def iota(shape, dim):
    return lax.broadcasted_iota(jnp.int32, shape, dim)


def xp(v):
    return pltpu.roll(v, v.shape[1] - 1, 1)


def xm(v):
    return pltpu.roll(v, 1, 1)


def yp(v):
    return pltpu.roll(v, v.shape[0] - 1, 0)


def ym(v):
    return pltpu.roll(v, 1, 0)


def split(v):
    high = v.astype(BF16)
    return high, (v - high.astype(F32)).astype(BF16)


def dot(a, b, precision=None):
    return jnp.dot(a, b, preferred_element_type=F32, precision=precision)


def make_kernel(zl, yl, ng, ny, factor):
    nv = yl // 8
    yr = yl + 2 * R
    n_core = 2 if ny % 2 == 0 else 1
    n_z = 8 if ng % 8 == 0 else 1
    size1 = n_core * n_z
    size2 = (ny // n_core) * (ng // n_z)

    def kernel(
        conc, cot, w_in, b_in, w_out, b_out,
        out, out_sums,
        C, A0, MU1, M1, SG1, C2, MU2, M2, SG2, RR, UU, VV, A1, GS, H1, H2,
        WL, WOF, CT, UB, PACC, TACC, GACC, OUTV, RED, RED2, MSG, MSG2,
        send_sem, recv_sem, local_sem, rs_send, rs_recv, rs2_send, rs2_recv,
    ):
        gz = lax.axis_index("gz")
        gy = lax.axis_index("gy")

        def neighbour(dz, dy):
            return (lax.rem(gz + dz + ng, ng), lax.rem(gy + dy + ny, ny))

        place1 = lax.rem(gy, n_core) * n_z + lax.rem(gz, n_z)
        place2 = (gy // n_core) * (ng // n_z) + gz // n_z

        def peer1(k):
            q = lax.rem(place1 + k, size1)
            return q, (gz // n_z * n_z + lax.rem(q, n_z), gy // n_core * n_core + q // n_z)

        def peer2(k):
            q = lax.rem(place2 + k, size2)
            outer = ng // n_z
            return q, (lax.rem(q, outer) * n_z + lax.rem(gz, n_z), q // outer * n_core + lax.rem(gy, n_core))

        local_c = pltpu.make_async_copy(
            conc, C.at[pl.ds(WC, zl), pl.ds(R, yl)], local_sem.at[0])
        local_a = pltpu.make_async_copy(
            cot, A0.at[pl.ds(WA, zl), pl.ds(R, yl)], local_sem.at[1])
        local_c.start()
        local_a.start()

        barrier = pltpu.get_barrier_semaphore()
        count = 0
        for dz, dy in DIRECTIONS:
            pl.semaphore_signal(barrier, inc=1, device_id=neighbour(dz, dy), device_id_type=MESH)
            count += 1
        for k in range(1, size1):
            pl.semaphore_signal(barrier, inc=1, device_id=peer1(k)[1], device_id_type=MESH)
            count += 1
        for k in range(1, size2):
            pl.semaphore_signal(barrier, inc=1, device_id=peer2(k)[1], device_id_type=MESH)
            count += 1
        pl.semaphore_wait(barrier, count)

        def span_z(dz, width):
            if dz > 0:
                return pl.ds(zl - width, width), pl.ds(0, width)
            if dz < 0:
                return pl.ds(0, width), pl.ds(width + zl, width)
            return pl.ds(0, zl), pl.ds(width, zl)

        def span_y(dy):
            if dy > 0:
                return pl.ds(yl - R, R), pl.ds(0, R)
            if dy < 0:
                return pl.ds(0, R), pl.ds(R + yl, R)
            return pl.ds(0, yl), pl.ds(R, yl)

        def halo(which, source, field, width):
            copies = {}
            for n, (dz, dy) in enumerate(DIRECTIONS):
                sz, tz = span_z(dz, width)
                sy, ty = span_y(dy)
                copies[dz, dy] = pltpu.make_async_remote_copy(
                    src_ref=source.at[sz, sy],
                    dst_ref=field.at[tz, ty],
                    send_sem=send_sem.at[which, n],
                    recv_sem=recv_sem.at[which, n],
                    device_id=neighbour(dz, dy),
                    device_id_type=MESH,
                )
            return copies

        halo_c = halo(0, conc, C, WC)
        halo_a = halo(1, cot, A0, WA)
        for copy in [*halo_c.values(), *halo_a.values()]:
            copy.start()

        lane = iota((UNITS, 128), 1)
        eye = iota((UNITS, UNITS), 0) == iota((UNITS, UNITS), 1)
        bi_col = jnp.sum(jnp.where(eye, b_in[...], 0.0), axis=1, keepdims=True)
        wo_col = jnp.sum(jnp.where(eye, w_out[...], 0.0), axis=1, keepdims=True)
        packed = jnp.where(lane == 4, bi_col, jnp.where(lane == 5, wo_col, 0.0))
        for k in range(4):
            w_col = jnp.sum(jnp.where(eye, w_in[k:k + 1, :], 0.0), axis=1, keepdims=True)
            packed = jnp.where(lane == k, w_col, packed)
        spread = (iota((ROWS, UNITS), 0) // 8 == iota((ROWS, UNITS), 1)).astype(F32)
        params = dot(spread, packed, HIGH)
        row = iota((ROWS, 128), 0)
        col = iota((ROWS, 128), 1)
        same = (row & 7) == (col & 7)
        which_k = (col & 31) // 8
        group = col // 32
        w_sel = jnp.zeros((ROWS, 128), F32)
        for k in range(4):
            w_sel = jnp.where(which_k == k, params[:, k:k + 1], w_sel)
        bias = jnp.broadcast_to(params[:, 4:5], (ROWS, 128))
        wo_full = jnp.broadcast_to(params[:, 5:6], (ROWS, 128))
        WOF[...] = wo_full
        value = jnp.where(group == 3, jnp.where(which_k < 2, bias, 0.0), w_sel)
        high = value.astype(BF16).astype(F32)
        low = value - high
        is_low = (group == 1) | ((group == 3) & (which_k == 1))
        WL[...] = jnp.where(same, jnp.where(is_low, low, high), 0.0).astype(BF16)
        joint = w_sel * wo_full
        j_high = joint.astype(BF16).astype(F32)
        j_low = joint - j_high
        j_mat = jnp.where(same, jnp.where(group == 0, j_high, jnp.where(group == 1, j_low, 0.0)), 0.0)
        CT[...] = j_mat.T[0:64].astype(BF16)
        PACC[...] = jnp.zeros((2 * ROWS, 128), F32)
        TACC[...] = jnp.zeros((ROWS, 128), F32)
        GACC[...] = jnp.zeros((8, 128), F32)

        half = iota((8, 128), 0) < 4

        def pack(v):
            blocks = [v[R + 8 * i:R + 8 * i + 8] for i in range(nv)]
            blocks.append(jnp.where(half, v[R + yl:], v[:R]))
            return blocks

        def unpack(blocks):
            return jnp.concatenate([blocks[-1]] + blocks[:-1] + [blocks[-1]], axis=0)

        def fields_of(c_ref, p):
            c = c_ref[p]
            zu, zd = c_ref[p + 1], c_ref[p - 1]
            yu, yd = yp(c), ym(c)
            xu, xd = xp(c), xm(c)
            lap = ((zu + zd) + (yu + yd)) + (xu + xd) - 6.0 * c
            s0, s1, s2 = 0.5 * (zu - zd), 0.5 * (yu - yd), 0.5 * (xu - xd)
            sq = s0 * s0 + s1 * s1 + s2 * s2
            return c, lap, sq, (s0, s1, s2)

        def units(pair):
            feats = jnp.concatenate([jnp.concatenate(f, axis=0) for f in pair], axis=1)
            f_high, f_low = split(feats)
            rhs = jnp.concatenate([f_high, f_high, f_low, jnp.ones((32, 256), BF16)], axis=0)
            return jnp.tanh(dot(WL[...], rhs))

        def score(h):
            wo = WOF[...]
            weighted = h * jnp.concatenate([wo, wo], axis=1)
            return jnp.sum(weighted.reshape(UNITS, 8, 256), axis=0) + b_out[0, 0]

        def soft(s):
            e = jnp.exp(s)
            return jnp.log(1.0 + e) + FLOOR, e / (1.0 + e)

        def forward_one(planes):
            for q in planes:
                c, lap, sq, _ = fields_of(C, q)
                mu = c * c * c - c - KAPPA * lap
                MU1[q] = mu
                feats = [c, lap, sq, mu]
                for a in range(0, nv + 2, 2):
                    ids = [1 + a, 2 + a] if a < nv else [nv + 1, 0]
                    pair = [[f[8 * i:8 * i + 8] for f in feats] for i in ids]
                    h = units(pair)
                    if a < nv:
                        H1[q, a] = h[:, :128]
                        H1[q, a + 1] = h[:, 128:]
                    else:
                        mask = (iota((ROWS, 128), 0) & 7) < 4
                        H1[q, nv] = jnp.where(mask, h[:, :128], h[:, 128:])
                    m, sg = soft(score(h))
                    for i in range(2):
                        rows = pl.ds(8 * ids[i], 8)
                        M1[q, rows] = m[:, 128 * i:128 * i + 128]
                        SG1[q, rows] = sg[:, 128 * i:128 * i + 128]

        def wait_for(copies, sides):
            for dz, dy in DIRECTIONS:
                if (dz == 0) == (sides == "y"):
                    copies[dz, dy].wait_recv()

        low, high = WC, WC + zl - 1

        def inner(width, body):
            for p in range(low + width, high - width, 2):
                body((p, p + 1))

        def outer(first, last, body):
            for k in range(-first, last):
                body((low - 1 - k, high + 1 + k))

        def advance(planes):
            for p in planes:
                advance_plane(p)

        def advance_plane(p):
            mu, m = MU1[p], M1[p]
            def face(mu_a, m_a, mu_b, m_b):
                return (m_a + m_b) * (mu_b - mu_a)
            up = face(mu, m, MU1[p + 1], M1[p + 1])
            down = face(MU1[p - 1], M1[p - 1], mu, m)
            fy = face(mu, m, yp(mu), yp(m))
            fx = face(mu, m, xp(mu), xp(m))
            total = (up - down) + (fy - ym(fy)) + (fx - xm(fx))
            C2[p] = C[p] + (0.5 * STEP) * total

        def forward_two(planes):
            feats = []
            for q in planes:
                c, lap, sq, _ = fields_of(C2, q)
                mu = c * c * c - c - KAPPA * lap
                MU2[q] = mu
                feats.append([pack(f) for f in (c, lap, sq, mu)])
            work = [((d, a), (d, a + 1)) for d in range(2) for a in range(0, nv, 2)] + [((0, nv), (1, nv))]
            for places in work:
                h = units([[f[a] for f in feats[d]] for d, a in places])
                m, sg = soft(score(h))
                for i, (d, a) in enumerate(places):
                    q = planes[d]
                    H2[q, a] = h[:, 128 * i:128 * i + 128]
                    mi, si = m[:, 128 * i:128 * i + 128], sg[:, 128 * i:128 * i + 128]
                    for start in ([R + 8 * a] if a < nv else [0, R + yl]):
                        M2[q, pl.ds(start, 8)] = mi
                        SG2[q, pl.ds(start, 8)] = si

        def faces(field, adj, shift, q, of):
            v, a = field[q], adj[q + shift]
            up = of(v, field[q + 1], adj[q + 1 + shift] - a)
            down = of(field[q - 1], v, a - adj[q - 1 + shift])
            fy = of(v, yp(v), yp(a) - a)
            fx = of(v, xp(v), xp(a) - a)
            return (up, down), (fy, ym(fy)), (fx, xm(fx))

        def score_adjoint(q, adj, shift, mu_ref, sg_ref):
            z, y, x = faces(mu_ref, adj, shift, q, lambda here, there, da: (there - here) * da)
            adj_mob = (z[0] + z[1]) + (y[0] + y[1]) + (x[0] + x[1])
            return (-0.5 * STEP) * adj_mob * sg_ref[q]

        def flux_adjoint(q, adj, shift, m_ref):
            z, y, x = faces(m_ref, adj, shift, q, lambda here, there, da: (here + there) * da)
            return (0.5 * STEP) * ((z[0] - z[1]) + (y[0] - y[1]) + (x[0] - x[1]))

        def places_of(with_core, with_sides):
            core = [((d, b), (d, b + 1)) for d in range(2) for b in range(0, nv, 2)] if with_core else []
            return core + ([((0, nv), (1, nv))] if with_sides else [])

        def hidden(planes, places, h_ref):
            h = jnp.concatenate([h_ref[planes[d], b] for d, b in places], axis=1)
            return 1.0 - h * h

        def sums(planes, g, c_ref, mu_ref, h_ref, ub):
            feats = []
            for q in planes:
                c, lap, sq, _ = fields_of(c_ref, q)
                feats.append([pack(f) for f in (c, lap, sq, mu_ref[q])])
            gg = []
            for n, places in enumerate(places_of(True, False)):
                u = hidden(planes, places, h_ref)
                u_high, u_low = split(u)
                ub[pl.ds(0, ROWS), pl.ds(256 * n, 256)] = u_high
                ub[pl.ds(ROWS, ROWS), pl.ds(256 * n, 256)] = u_low
                gs = jnp.concatenate([g[d][b] for d, b in places], axis=1)
                stack = [gs * jnp.concatenate([feats[d][k][b] for d, b in places], axis=1) for k in range(4)]
                s_high, s_low = split(jnp.concatenate(stack + [gs, jnp.zeros((8, 256), F32)], axis=0))
                gg.append(jnp.concatenate([s_high, s_low, jnp.zeros((32, 256), BF16)], axis=0))
            PACC[...] += lax.dot_general(
                ub[...], jnp.concatenate(gg, axis=1), (((1,), (1,)), ((), ())), preferred_element_type=F32)
            total = TACC[...].reshape(UNITS, 8, 128)
            g_total = GACC[...]
            for d in range(2):
                for b in range(nv):
                    total = total + h_ref[planes[d], b].reshape(UNITS, 8, 128) * g[d][b][None]
                    g_total = g_total + g[d][b]
            TACC[...] = total.reshape(ROWS, 128)
            GACC[...] = g_total

        def finish(planes, g, adj, shift, c_ref, m_ref, h_ref):
            A = [[None] * (nv + 1) for _ in planes]
            for places in places_of(True, True):
                back = dot(CT[...], hidden(planes, places, h_ref).astype(BF16))
                back = back[:32] + back[32:]
                for i, (d, b) in enumerate(places):
                    A[d][b] = [back[8 * k:8 * k + 8, 128 * i:128 * i + 128] * g[d][b] for k in range(4)]
            for d, q in enumerate(planes):
                a_c, a_lap, a_sq, a_mu = (unpack([A[d][b][k] for b in range(nv + 1)]) for k in range(4))
                c, _, _, slopes = fields_of(c_ref, q)
                adj_pot = flux_adjoint(q, adj, shift, m_ref) + a_mu
                adj_lap = a_lap - KAPPA * adj_pot
                zed, why, ex = (a_sq * slope for slope in slopes)
                rest = adj[q + shift] + a_c + (3.0 * c * c - 1.0) * adj_pot - 6.0 * adj_lap
                rest = rest + (xm(adj_lap + ex) + xp(adj_lap - ex)) + (ym(adj_lap + why) + yp(adj_lap - why))
                RR[q] = rest
                UU[q] = adj_lap + zed
                VV[q] = adj_lap - zed

        turn = [0]

        def buffer():
            turn[0] ^= 1
            return UB.at[turn[0]]

        def back_two(with_sums):
            def body(planes):
                g = [pack(score_adjoint(q, A0, WA - WC, MU2, SG2)) for q in planes]
                if with_sums:
                    sums(planes, g, C2, MU2, H2, buffer())
                finish(planes, g, A0, WA - WC, C2, M2, H2)
            return body

        def back_one_sums(planes):
            g = [pack(score_adjoint(q, A1, 0, MU1, SG1)) for q in planes]
            sums(planes, g, C, MU1, H1, buffer())
            for d, q in enumerate(planes):
                for b in range(nv + 1):
                    GS[q, pl.ds(8 * b, 8)] = g[d][b]

        def back_one_rest(planes):
            g = [[GS[q, pl.ds(8 * b, 8)] for b in range(nv + 1)] for q in planes]
            finish(planes, g, A1, 0, C, M1, H1)

        def back_one_sides(planes):
            g = [pack(score_adjoint(q, A1, 0, MU1, SG1)) for q in planes]
            finish(planes, g, A1, 0, C, M1, H1)

        def join(p):
            A1[p] = RR[p] + UU[p - 1] + VV[p + 1]

        local_c.wait()
        wait_for(halo_c, "y")
        inner(1, forward_one)
        inner(2, advance)
        inner(3, forward_two)
        local_a.wait()
        wait_for(halo_a, "y")
        inner(4, back_two(True))
        wait_for(halo_c, "z")
        outer(1, 6, forward_one)
        outer(2, 5, advance)
        outer(3, 4, forward_two)
        wait_for(halo_a, "z")
        outer(4, 0, back_two(True))
        outer(0, 3, back_two(False))
        for p in range(low - 2, high + 3):
            join(p)
        inner(0, back_one_sums)

        both = PACC[pl.ds(0, ROWS)] + PACC[pl.ds(ROWS, ROWS)]
        both = jnp.where(same & (col < 96), both, 0.0)
        gather = (iota((UNITS, ROWS), 1) // 8 == iota((UNITS, ROWS), 0)).astype(F32)
        by_unit = dot(gather, both, HIGH)
        c_row = iota((128, 128), 0)
        c_col = iota((128, 128), 1)
        c_k = jnp.where(c_row < 48, c_row, c_row - 48) // 8
        collect = ((c_k == c_col) & (c_row < 96) & (c_col < 5)).astype(F32)
        grads = dot(by_unit, collect, HIGH) * wo_col
        t_col = jnp.sum(dot(gather, TACC[...], HIGH), axis=1, keepdims=True)
        g_sum = jnp.sum(jnp.sum(GACC[...], axis=0, keepdims=True), axis=1, keepdims=True)
        first_row = iota((UNITS, 128), 0) == 0
        grads = jnp.where(lane == 5, t_col, grads)
        grads = jnp.where((lane == 6) & first_row, g_sum, grads)
        square = jnp.concatenate([grads, jnp.zeros((128 - UNITS, 128), F32)], axis=0)
        MSG[...] = square.T[0:8]

        def exchange(size, place, peer, src, slots, s_sem, r_sem):
            copies = []
            for k in range(1, size):
                q, device = peer(k)
                copy = pltpu.make_async_remote_copy(
                    src_ref=src, dst_ref=slots.at[place], send_sem=s_sem.at[k],
                    recv_sem=r_sem.at[place], device_id=device, device_id_type=MESH)
                copy.start()
                copies.append(copy)
            slots[place] = src[...]
            return copies

        def collected(size, peer, copies, src, slots, s_sem, r_sem):
            for k in range(1, size):
                q, device = peer(k)
                pltpu.make_async_remote_copy(
                    src_ref=src, dst_ref=slots.at[q], send_sem=s_sem.at[k],
                    recv_sem=r_sem.at[q], device_id=device, device_id_type=MESH).wait_recv()
            total = slots[0]
            for k in range(1, size):
                total = total + slots[k]
            return total

        sent1 = exchange(size1, place1, peer1, MSG, RED, rs_send, rs_recv)

        outer(0, 1, back_one_sides)
        inner(0, back_one_rest)
        for p in range(low, high + 1):
            rows = pl.ds(R, yl)
            OUTV[p - WC] = RR[p, rows] + UU[p - 1, rows] + VV[p + 1, rows]
        write = pltpu.make_async_copy(OUTV, out, local_sem.at[2])
        write.start()

        total = collected(size1, peer1, sent1, MSG, RED, rs_send, rs_recv)
        MSG2[...] = total
        if size2 > 1:
            sent2 = exchange(size2, place2, peer2, MSG2, RED2, rs2_send, rs2_recv)
            total = collected(size2, peer2, sent2, MSG2, RED2, rs2_send, rs2_recv)
        else:
            sent2 = []
        out_sums[...] = total * factor

        for copy in [*halo_c.values(), *halo_a.values(), *sent1, *sent2]:
            copy.wait_send()
        write.wait()

    return kernel, yr, size1, size2


def hand_over(field, sums, out, out_wi, out_bi, out_wo, out_bo, sem):
    copy = pltpu.make_async_copy(field, out, sem)
    copy.start()
    out_wi[...] = sums[0:4, 0:UNITS]
    out_bi[...] = sums[4:5, 0:UNITS]
    out_wo[...] = sums[5:6, 0:UNITS]
    out_bo[...] = sums[6:7, 0:1]
    copy.wait()


def per_device(ng, ny, concentration, cotangent, w_in, b_in, w_out, b_out):
    zl, yl, nx = concentration.shape
    factor = 1.0 / (STEP * math.sqrt(float(zl * yl * nx * ng * ny)))
    kernel, yr, size1, size2 = make_kernel(zl, yl, ng, ny, factor)
    planes = zl + 2 * WC
    nv = yl // 8
    field = pltpu.VMEM((planes, yr, nx), F32)
    anywhere = pl.BlockSpec(memory_space=pl.ANY)
    vmem = pl.BlockSpec(memory_space=pltpu.VMEM)
    smem = pl.BlockSpec(memory_space=pltpu.SMEM)
    outs = pl.pallas_call(
        kernel,
        out_shape=(
            jax.ShapeDtypeStruct(concentration.shape, F32),
            jax.ShapeDtypeStruct((8, 128), F32),
        ),
        in_specs=[anywhere, anywhere, vmem, vmem, vmem, smem],
        out_specs=(anywhere, vmem),
        scratch_shapes=[
            field,
            pltpu.VMEM((zl + 2 * WA, yr, nx), F32),
            field, field, field,
            field, field, field, field,
            field, field, field, field,
            pltpu.VMEM((planes, yl + 8, nx), F32),
            pltpu.VMEM((planes, nv + 1, ROWS, nx), F32),
            pltpu.VMEM((planes, nv + 1, ROWS, nx), F32),
            pltpu.VMEM((ROWS, 128), BF16),
            pltpu.VMEM((ROWS, 128), F32),
            pltpu.VMEM((64, ROWS), BF16),
            pltpu.VMEM((2, 2 * ROWS, 2 * yl // 8 * 128), BF16),
            pltpu.VMEM((2 * ROWS, 128), F32),
            pltpu.VMEM((ROWS, 128), F32),
            pltpu.VMEM((8, 128), F32),
            pltpu.VMEM((zl, yl, nx), F32),
            pltpu.VMEM((size1, 8, 128), F32),
            pltpu.VMEM((max(size2, 1), 8, 128), F32),
            pltpu.VMEM((8, 128), F32),
            pltpu.VMEM((8, 128), F32),
            pltpu.SemaphoreType.DMA((2, 8)),
            pltpu.SemaphoreType.DMA((2, 8)),
            pltpu.SemaphoreType.DMA((3,)),
            pltpu.SemaphoreType.DMA((size1,)),
            pltpu.SemaphoreType.DMA((size1,)),
            pltpu.SemaphoreType.DMA((size2,)),
            pltpu.SemaphoreType.DMA((size2,)),
        ],
        compiler_params=pltpu.CompilerParams(
            collective_id=0, has_side_effects=True, vmem_limit_bytes=60 * 1024 * 1024
        ),
    )(
        concentration, cotangent, w_in.T, b_in.reshape(1, UNITS), w_out.reshape(1, UNITS), b_out.reshape(1, 1)
    )
    outs = pl.pallas_call(
        hand_over,
        out_shape=(
            jax.ShapeDtypeStruct(concentration.shape, F32),
            jax.ShapeDtypeStruct((4, UNITS), F32),
            jax.ShapeDtypeStruct((1, UNITS), F32),
            jax.ShapeDtypeStruct((1, UNITS), F32),
            jax.ShapeDtypeStruct((1, 1), F32),
        ),
        in_specs=[anywhere, vmem],
        out_specs=(anywhere, vmem, vmem, vmem, vmem),
        scratch_shapes=[pltpu.SemaphoreType.DMA],
    )(*outs)
    return (outs[0], outs[1].T, outs[2].reshape(UNITS), outs[3].reshape(UNITS), outs[4].reshape(()))


def solution(mesh):
    ng, ny = mesh.shape["gz"], mesh.shape["gy"]
    in_specs = (P("gz", "gy", None), P("gz", "gy", None), P(), P(), P(), P())
    out_specs = (P("gz", "gy", None), P(), P(), P(), P())

    def run(*args):
        return per_device(ng, ny, *args)

    return jax.shard_map(run, mesh=mesh, in_specs=in_specs, out_specs=out_specs, check_vma=False)
```

```python
import math

import jax
import jax.numpy as jnp
from jax import lax
from jax.experimental import pallas as pl
from jax.experimental.pallas import tpu as pltpu
from jax.sharding import PartitionSpec as P

KAPPA = 0.5
STEP = 0.008
FLOOR = 0.05
HIGH = lax.Precision.HIGHEST
MESH = pl.DeviceIdType.MESH
F32 = jnp.float32
BF16 = jnp.bfloat16

WC = 7
WA = 4
R = 8
UNITS = 32
ROWS = UNITS * 8


DIRECTIONS = [(dz, dy) for dz in (0, -1, 1) for dy in (-1, 1, 0) if (dz, dy) != (0, 0)]

CORNER_C = ((0, 2, 8), (2, 4, 4))
CORNER_A = ((0, 3, 4),)
PIECES_C = [(dz, dy, n) for dz, dy in DIRECTIONS for n in range(len(CORNER_C) if dz * dy else 1)]
PIECES_A = [(dz, dy, n) for dz, dy in DIRECTIONS for n in range(len(CORNER_A) if dz * dy else 1)]


def iota(shape, dim):
    return lax.broadcasted_iota(jnp.int32, shape, dim)


def xp(v):
    return pltpu.roll(v, v.shape[1] - 1, 1)


def xm(v):
    return pltpu.roll(v, 1, 1)


def yp(v):
    return pltpu.roll(v, v.shape[0] - 1, 0)


def ym(v):
    return pltpu.roll(v, 1, 0)


def split(v):
    high = v.astype(BF16)
    return high, (v - high.astype(F32)).astype(BF16)


def dot(a, b, precision=None):
    return jnp.dot(a, b, preferred_element_type=F32, precision=precision)


def make_kernel(zl, yl, ng, ny, factor):
    nv = yl // 8
    yr = yl + 2 * R
    n_core = 2 if ny % 2 == 0 else 1
    n_z = 8 if ng % 8 == 0 else 1
    size1 = n_core * n_z
    size2 = (ny // n_core) * (ng // n_z)

    def kernel(
        conc, cot, w_in, b_in, w_out, b_out,
        out, out_sums,
        C, A0, MU1, M1, SG1, C2, MU2, M2, SG2, RR, UU, VV, A1, GS, H1, H2,
        WL, WOF, CT, UB, PACC, TACC, GACC, OUTV, RED, RED2, MSG, MSG2,
        send_sem, recv_sem, local_sem, rs_send, rs_recv, rs2_send, rs2_recv,
    ):
        gz = lax.axis_index("gz")
        gy = lax.axis_index("gy")

        def neighbour(dz, dy):
            return (lax.rem(gz + dz + ng, ng), lax.rem(gy + dy + ny, ny))

        place1 = lax.rem(gy, n_core) * n_z + lax.rem(gz, n_z)
        place2 = (gy // n_core) * (ng // n_z) + gz // n_z

        def peer1(k):
            q = lax.rem(place1 + k, size1)
            return q, (gz // n_z * n_z + lax.rem(q, n_z), gy // n_core * n_core + q // n_z)

        def peer2(k):
            q = lax.rem(place2 + k, size2)
            outer = ng // n_z
            return q, (lax.rem(q, outer) * n_z + lax.rem(gz, n_z), q // outer * n_core + lax.rem(gy, n_core))

        local_c = pltpu.make_async_copy(
            conc, C.at[pl.ds(WC, zl), pl.ds(R, yl)], local_sem.at[0])
        local_a = pltpu.make_async_copy(
            cot, A0.at[pl.ds(WA, zl), pl.ds(R, yl)], local_sem.at[1])
        local_c.start()
        local_a.start()

        for margin in (0, R + yl):
            for first, length in ((0, WC - 2), (WC + zl + 2, WC - 2)):
                rows = pl.ds(margin + (0 if margin == 0 else 4), 4)
                C[pl.ds(first, length), rows] = jnp.zeros((length, 4, 128), F32)
            for p in (0, 2 * WC + zl - 1):
                C[p, pl.ds(margin, R)] = jnp.zeros((R, 128), F32)
            rows = pl.ds(margin + (0 if margin == 0 else 4), 4)
            A0[:, rows] = jnp.zeros((zl + 2 * WA, 4, 128), F32)
            for p in (0, 2 * WA + zl - 1):
                A0[p, pl.ds(margin, R)] = jnp.zeros((R, 128), F32)

        barrier = pltpu.get_barrier_semaphore()
        count = 0
        for dz, dy in DIRECTIONS:
            pl.semaphore_signal(barrier, inc=1, device_id=neighbour(dz, dy), device_id_type=MESH)
            count += 1
        for k in range(1, size1):
            pl.semaphore_signal(barrier, inc=1, device_id=peer1(k)[1], device_id_type=MESH)
            count += 1
        for k in range(1, size2):
            pl.semaphore_signal(barrier, inc=1, device_id=peer2(k)[1], device_id_type=MESH)
            count += 1
        pl.semaphore_wait(barrier, count)

        def span(d, size, edge, first, length):
            if d > 0:
                return pl.ds(size - first - length, length), pl.ds(edge - first - length, length)
            if d < 0:
                return pl.ds(first, length), pl.ds(edge + size + first, length)
            return pl.ds(0, size), pl.ds(edge, size)

        def halo(which, source, field, pieces, width, rows, corner):
            copies = {}
            for n, (dz, dy, part) in enumerate(pieces):
                first, planes, high_rows = corner[part] if dz * dy else (0, width, rows)
                sz, tz = span(dz, zl, width, first, planes)
                sy, ty = span(dy, yl, R, 0, high_rows)
                copies[dz, dy, part] = pltpu.make_async_remote_copy(
                    src_ref=source.at[sz, sy],
                    dst_ref=field.at[tz, ty],
                    send_sem=send_sem.at[which, n],
                    recv_sem=recv_sem.at[which, n],
                    device_id=neighbour(dz, dy),
                    device_id_type=MESH,
                )
            return copies

        halo_c = halo(0, conc, C, PIECES_C, WC, 8, CORNER_C)
        halo_a = halo(1, cot, A0, PIECES_A, WA, 4, CORNER_A)
        for copy in halo_c.values():
            copy.start()
        for dy in (-1, 1):
            halo_a[0, dy, 0].start()

        lane = iota((UNITS, 128), 1)
        eye = iota((UNITS, UNITS), 0) == iota((UNITS, UNITS), 1)
        bi_col = jnp.sum(jnp.where(eye, b_in[...], 0.0), axis=1, keepdims=True)
        wo_col = jnp.sum(jnp.where(eye, w_out[...], 0.0), axis=1, keepdims=True)
        packed = jnp.where(lane == 4, bi_col, jnp.where(lane == 5, wo_col, 0.0))
        for k in range(4):
            w_col = jnp.sum(jnp.where(eye, w_in[k:k + 1, :], 0.0), axis=1, keepdims=True)
            packed = jnp.where(lane == k, w_col, packed)
        spread = (iota((ROWS, UNITS), 0) // 8 == iota((ROWS, UNITS), 1)).astype(F32)
        params = dot(spread, packed, HIGH)
        row = iota((ROWS, 128), 0)
        col = iota((ROWS, 128), 1)
        same = (row & 7) == (col & 7)
        which_k = (col & 31) // 8
        group = col // 32
        w_sel = jnp.zeros((ROWS, 128), F32)
        for k in range(4):
            w_sel = jnp.where(which_k == k, params[:, k:k + 1], w_sel)
        bias = jnp.broadcast_to(params[:, 4:5], (ROWS, 128))
        wo_full = jnp.broadcast_to(params[:, 5:6], (ROWS, 128))
        WOF[...] = wo_full
        value = jnp.where(group == 3, jnp.where(which_k < 2, bias, 0.0), w_sel)
        high = value.astype(BF16).astype(F32)
        low = value - high
        is_low = (group == 1) | ((group == 3) & (which_k == 1))
        WL[...] = jnp.where(same, jnp.where(is_low, low, high), 0.0).astype(BF16)
        joint = w_sel * wo_full
        j_high = joint.astype(BF16).astype(F32)
        j_low = joint - j_high
        j_mat = jnp.where(same, jnp.where(group == 0, j_high, jnp.where(group == 1, j_low, 0.0)), 0.0)
        CT[...] = j_mat.T[0:64].astype(BF16)
        PACC[...] = jnp.zeros((2 * ROWS, 128), F32)
        TACC[...] = jnp.zeros((ROWS, 128), F32)
        GACC[...] = jnp.zeros((8, 128), F32)

        half = iota((8, 128), 0) < 4

        def pack(v):
            blocks = [v[R + 8 * i:R + 8 * i + 8] for i in range(nv)]
            blocks.append(jnp.where(half, v[R + yl:], v[:R]))
            return blocks

        def unpack(blocks):
            return jnp.concatenate([blocks[-1]] + blocks[:-1] + [blocks[-1]], axis=0)

        def fields_of(c_ref, p, rows=slice(None)):
            c = c_ref[p, rows]
            zu, zd = c_ref[p + 1, rows], c_ref[p - 1, rows]
            yu, yd = yp(c), ym(c)
            xu, xd = xp(c), xm(c)
            lap = ((zu + zd) + (yu + yd)) + (xu + xd) - 6.0 * c
            s0, s1, s2 = 0.5 * (zu - zd), 0.5 * (yu - yd), 0.5 * (xu - xd)
            sq = s0 * s0 + s1 * s1 + s2 * s2
            return c, lap, sq, (s0, s1, s2)

        def units(pair):
            feats = jnp.concatenate([jnp.concatenate(f, axis=0) for f in pair], axis=1)
            f_high, f_low = split(feats)
            rhs = jnp.concatenate([f_high, f_high, f_low, jnp.ones((32, 256), BF16)], axis=0)
            return jnp.tanh(dot(WL[...], rhs))

        def score(h):
            wo = WOF[...]
            weighted = h * jnp.concatenate([wo, wo], axis=1)
            return jnp.sum(weighted.reshape(UNITS, 8, 256), axis=0) + b_out[0, 0]

        def soft(s):
            e = jnp.exp(s)
            return jnp.log(1.0 + e) + FLOOR, e / (1.0 + e)

        def forward_blocks(q, feats, ids, offset):
            pair = [[f[8 * i - offset:8 * i - offset + 8] for f in feats] for i in ids]
            h = units(pair)
            if ids[0] > nv:
                mask = (iota((ROWS, 128), 0) & 7) < 4
                H1[q, nv] = jnp.where(mask, h[:, :128], h[:, 128:])
            else:
                for i in range(2):
                    H1[q, ids[i] - 1] = h[:, 128 * i:128 * i + 128]
            m, sg = soft(score(h))
            for i in range(2):
                rows = pl.ds(8 * ids[i], 8)
                M1[q, rows] = m[:, 128 * i:128 * i + 128]
                SG1[q, rows] = sg[:, 128 * i:128 * i + 128]

        def forward_one_early(planes):
            for q in planes:
                c, lap, sq, _ = fields_of(C, q, pl.ds(R, yl))
                feats = [c, lap, sq, c * c * c - c - KAPPA * lap]
                for i in range(2, nv, 2):
                    forward_blocks(q, feats, (i, i + 1), R)

        def forward_one(planes, early=False):
            for q in planes:
                c, lap, sq, _ = fields_of(C, q)
                mu = c * c * c - c - KAPPA * lap
                MU1[q] = mu
                feats = [c, lap, sq, mu]
                if not early:
                    for i in range(2, nv, 2):
                        forward_blocks(q, feats, (i, i + 1), 0)
                forward_blocks(q, feats, (1, nv), 0)
                forward_blocks(q, feats, (nv + 1, 0), 0)

        def wait_for(copies, sides):
            for dz, dy, part in copies:
                if (dz == 0) == (sides == "y"):
                    copies[dz, dy, part].wait_recv()

        low, high = WC, WC + zl - 1

        def inner(width, body):
            for p in range(low + width, high - width, 2):
                body((p, p + 1))

        def outer(first, last, body):
            for k in range(-first, last):
                body((low - 1 - k, high + 1 + k))

        def advance(planes):
            for p in planes:
                advance_plane(p)

        def advance_plane(p):
            mu, m = MU1[p], M1[p]
            def face(mu_a, m_a, mu_b, m_b):
                return (m_a + m_b) * (mu_b - mu_a)
            up = face(mu, m, MU1[p + 1], M1[p + 1])
            down = face(MU1[p - 1], M1[p - 1], mu, m)
            fy = face(mu, m, yp(mu), yp(m))
            fx = face(mu, m, xp(mu), xp(m))
            total = (up - down) + (fy - ym(fy)) + (fx - xm(fx))
            C2[p] = C[p] + (0.5 * STEP) * total

        def forward_two(planes):
            feats = []
            for q in planes:
                c, lap, sq, _ = fields_of(C2, q)
                mu = c * c * c - c - KAPPA * lap
                MU2[q] = mu
                feats.append([pack(f) for f in (c, lap, sq, mu)])
            work = [((d, a), (d, a + 1)) for d in range(2) for a in range(0, nv, 2)] + [((0, nv), (1, nv))]
            for places in work:
                h = units([[f[a] for f in feats[d]] for d, a in places])
                m, sg = soft(score(h))
                for i, (d, a) in enumerate(places):
                    q = planes[d]
                    H2[q, a] = h[:, 128 * i:128 * i + 128]
                    mi, si = m[:, 128 * i:128 * i + 128], sg[:, 128 * i:128 * i + 128]
                    for start in ([R + 8 * a] if a < nv else [0, R + yl]):
                        M2[q, pl.ds(start, 8)] = mi
                        SG2[q, pl.ds(start, 8)] = si

        def jumps(q, adj, shift):
            a = adj[q + shift]
            return adj[q + 1 + shift] - a, a - adj[q - 1 + shift], yp(a) - a, xp(a) - a

        def faces(field, q, da, of):
            v = field[q]
            up = of(v, field[q + 1], da[0])
            down = of(field[q - 1], v, da[1])
            fy = of(v, yp(v), da[2])
            fx = of(v, xp(v), da[3])
            return (up, down), (fy, ym(fy)), (fx, xm(fx))

        def score_adjoint(q, da, mu_ref, sg_ref):
            z, y, x = faces(mu_ref, q, da, lambda here, there, d: (there - here) * d)
            adj_mob = (z[0] + z[1]) + (y[0] + y[1]) + (x[0] + x[1])
            return (-0.5 * STEP) * adj_mob * sg_ref[q]

        def flux_adjoint(q, da, m_ref):
            z, y, x = faces(m_ref, q, da, lambda here, there, d: (here + there) * d)
            return (0.5 * STEP) * ((z[0] - z[1]) + (y[0] - y[1]) + (x[0] - x[1]))

        def places_of(with_core, with_sides):
            core = [((d, b), (d, b + 1)) for d in range(2) for b in range(0, nv, 2)] if with_core else []
            return core + ([((0, nv), (1, nv))] if with_sides else [])

        def hidden(planes, places, h_ref):
            h = jnp.concatenate([h_ref[planes[d], b] for d, b in places], axis=1)
            return 1.0 - h * h

        def sums(planes, g, local, mu_ref, h_ref, ub):
            feats = []
            for q, (c, lap, sq, _) in zip(planes, local):
                feats.append([pack(f) for f in (c, lap, sq, mu_ref[q])])
            gg = []
            for n, places in enumerate(places_of(True, False)):
                u = hidden(planes, places, h_ref)
                u_high, u_low = split(u)
                ub[pl.ds(0, ROWS), pl.ds(256 * n, 256)] = u_high
                ub[pl.ds(ROWS, ROWS), pl.ds(256 * n, 256)] = u_low
                gs = jnp.concatenate([g[d][b] for d, b in places], axis=1)
                stack = [gs * jnp.concatenate([feats[d][k][b] for d, b in places], axis=1) for k in range(4)]
                s_high, s_low = split(jnp.concatenate(stack + [gs, jnp.zeros((8, 256), F32)], axis=0))
                gg.append(jnp.concatenate([s_high, s_low, jnp.zeros((32, 256), BF16)], axis=0))
            PACC[...] += lax.dot_general(
                ub[...], jnp.concatenate(gg, axis=1), (((1,), (1,)), ((), ())), preferred_element_type=F32)
            total = TACC[...].reshape(UNITS, 8, 128)
            g_total = GACC[...]
            for d in range(2):
                for b in range(nv):
                    total = total + h_ref[planes[d], b].reshape(UNITS, 8, 128) * g[d][b][None]
                    g_total = g_total + g[d][b]
            TACC[...] = total.reshape(ROWS, 128)
            GACC[...] = g_total

        def finish(planes, g, steps, local, adj, shift, m_ref, h_ref):
            A = [[None] * (nv + 1) for _ in planes]
            for places in places_of(True, True):
                back = dot(CT[...], hidden(planes, places, h_ref).astype(BF16))
                back = back[:32] + back[32:]
                for i, (d, b) in enumerate(places):
                    A[d][b] = [back[8 * k:8 * k + 8, 128 * i:128 * i + 128] * g[d][b] for k in range(4)]
            for d, q in enumerate(planes):
                a_c, a_lap, a_sq, a_mu = (unpack([A[d][b][k] for b in range(nv + 1)]) for k in range(4))
                c, _, _, slopes = local[d]
                adj_pot = flux_adjoint(q, steps[d], m_ref) + a_mu
                adj_lap = a_lap - KAPPA * adj_pot
                zed, why, ex = (a_sq * slope for slope in slopes)
                rest = adj[q + shift] + a_c + (3.0 * c * c - 1.0) * adj_pot - 6.0 * adj_lap
                rest = rest + (xm(adj_lap + ex) + xp(adj_lap - ex)) + (ym(adj_lap + why) + yp(adj_lap - why))
                RR[q] = rest
                UU[q] = adj_lap + zed
                VV[q] = adj_lap - zed

        turn = [0]

        def buffer():
            turn[0] ^= 1
            return UB.at[turn[0]]

        def start_of(planes, adj, shift, c_ref):
            return [jumps(q, adj, shift) for q in planes], [fields_of(c_ref, q) for q in planes]

        def back_two(with_sums):
            def body(planes):
                shift = WA - WC
                steps, local = start_of(planes, A0, shift, C2)
                g = [pack(score_adjoint(q, da, MU2, SG2)) for q, da in zip(planes, steps)]
                if with_sums:
                    sums(planes, g, local, MU2, H2, buffer())
                finish(planes, g, steps, local, A0, shift, M2, H2)
            return body

        def back_one_sums(planes):
            steps, local = start_of(planes, A1, 0, C)
            g = [pack(score_adjoint(q, da, MU1, SG1)) for q, da in zip(planes, steps)]
            sums(planes, g, local, MU1, H1, buffer())
            for d, q in enumerate(planes):
                for b in range(nv + 1):
                    GS[q, pl.ds(8 * b, 8)] = g[d][b]

        def back_one_rest(planes):
            steps, local = start_of(planes, A1, 0, C)
            g = [[GS[q, pl.ds(8 * b, 8)] for b in range(nv + 1)] for q in planes]
            finish(planes, g, steps, local, A1, 0, M1, H1)

        def back_one_sides(planes):
            steps, local = start_of(planes, A1, 0, C)
            g = [pack(score_adjoint(q, da, MU1, SG1)) for q, da in zip(planes, steps)]
            finish(planes, g, steps, local, A1, 0, M1, H1)

        def join(p):
            A1[p] = RR[p] + UU[p - 1] + VV[p + 1]

        local_c.wait()
        inner(1, forward_one_early)
        wait_for(halo_c, "y")
        inner(1, lambda planes: forward_one(planes, True))
        inner(2, advance)
        inner(3, forward_two)
        local_a.wait()
        wait_for(halo_a, "y")
        for dz, dy, _ in PIECES_A:
            if dz != 0:
                halo_a[dz, dy, 0].start()
        inner(4, back_two(True))
        wait_for(halo_c, "z")
        outer(1, 6, forward_one)
        outer(2, 5, advance)
        outer(3, 4, forward_two)
        wait_for(halo_a, "z")
        outer(4, 0, back_two(True))
        outer(0, 3, back_two(False))
        for p in range(low - 2, high + 3):
            join(p)
        inner(0, back_one_sums)

        both = PACC[pl.ds(0, ROWS)] + PACC[pl.ds(ROWS, ROWS)]
        both = jnp.where(same & (col < 96), both, 0.0)
        gather = (iota((UNITS, ROWS), 1) // 8 == iota((UNITS, ROWS), 0)).astype(F32)
        by_unit = dot(gather, both, HIGH)
        c_row = iota((128, 128), 0)
        c_col = iota((128, 128), 1)
        c_k = jnp.where(c_row < 48, c_row, c_row - 48) // 8
        collect = ((c_k == c_col) & (c_row < 96) & (c_col < 5)).astype(F32)
        grads = dot(by_unit, collect, HIGH) * wo_col
        t_col = jnp.sum(dot(gather, TACC[...], HIGH), axis=1, keepdims=True)
        g_sum = jnp.sum(jnp.sum(GACC[...], axis=0, keepdims=True), axis=1, keepdims=True)
        first_row = iota((UNITS, 128), 0) == 0
        grads = jnp.where(lane == 5, t_col, grads)
        grads = jnp.where((lane == 6) & first_row, g_sum, grads)
        square = jnp.concatenate([grads, jnp.zeros((128 - UNITS, 128), F32)], axis=0)
        MSG[...] = square.T[0:8]

        def exchange(size, place, peer, src, slots, s_sem, r_sem):
            copies = []
            for k in range(1, size):
                q, device = peer(k)
                copy = pltpu.make_async_remote_copy(
                    src_ref=src, dst_ref=slots.at[place], send_sem=s_sem.at[k],
                    recv_sem=r_sem.at[place], device_id=device, device_id_type=MESH)
                copy.start()
                copies.append(copy)
            slots[place] = src[...]
            return copies

        def collected(size, peer, copies, src, slots, s_sem, r_sem):
            for k in range(1, size):
                q, device = peer(k)
                pltpu.make_async_remote_copy(
                    src_ref=src, dst_ref=slots.at[q], send_sem=s_sem.at[k],
                    recv_sem=r_sem.at[q], device_id=device, device_id_type=MESH).wait_recv()
            total = slots[0]
            for k in range(1, size):
                total = total + slots[k]
            return total

        sent1 = exchange(size1, place1, peer1, MSG, RED, rs_send, rs_recv)

        outer(0, 1, back_one_sides)
        inner(0, back_one_rest)
        for p in range(low, high + 1):
            rows = pl.ds(R, yl)
            OUTV[p - WC] = RR[p, rows] + UU[p - 1, rows] + VV[p + 1, rows]
        write = pltpu.make_async_copy(OUTV, out, local_sem.at[2])
        write.start()

        total = collected(size1, peer1, sent1, MSG, RED, rs_send, rs_recv)
        MSG2[...] = total
        if size2 > 1:
            sent2 = exchange(size2, place2, peer2, MSG2, RED2, rs2_send, rs2_recv)
            total = collected(size2, peer2, sent2, MSG2, RED2, rs2_send, rs2_recv)
        else:
            sent2 = []
        out_sums[...] = total * factor

        for copy in [*halo_c.values(), *halo_a.values(), *sent1, *sent2]:
            copy.wait_send()
        write.wait()

    return kernel, yr, size1, size2


def hand_over(field, sums, out, out_wi, out_bi, out_wo, out_bo):
    out[...] = field[...]
    out_wi[...] = sums[0:4, 0:UNITS]
    out_bi[...] = sums[4:5, 0:UNITS]
    out_wo[...] = sums[5:6, 0:UNITS]
    out_bo[...] = sums[6:7, 0:1]


def per_device(ng, ny, concentration, cotangent, w_in, b_in, w_out, b_out):
    zl, yl, nx = concentration.shape
    factor = 1.0 / (STEP * math.sqrt(float(zl * yl * nx * ng * ny)))
    kernel, yr, size1, size2 = make_kernel(zl, yl, ng, ny, factor)
    planes = zl + 2 * WC
    nv = yl // 8
    field = pltpu.VMEM((planes, yr, nx), F32)
    anywhere = pl.BlockSpec(memory_space=pl.ANY)
    vmem = pl.BlockSpec(memory_space=pltpu.VMEM)
    smem = pl.BlockSpec(memory_space=pltpu.SMEM)
    outs = pl.pallas_call(
        kernel,
        out_shape=(
            jax.ShapeDtypeStruct(concentration.shape, F32),
            jax.ShapeDtypeStruct((8, 128), F32),
        ),
        in_specs=[anywhere, anywhere, vmem, vmem, vmem, smem],
        out_specs=(anywhere, vmem),
        scratch_shapes=[
            field,
            pltpu.VMEM((zl + 2 * WA, yr, nx), F32),
            field, field, field,
            field, field, field, field,
            field, field, field, field,
            pltpu.VMEM((planes, yl + 8, nx), F32),
            pltpu.VMEM((planes, nv + 1, ROWS, nx), F32),
            pltpu.VMEM((planes, nv + 1, ROWS, nx), F32),
            pltpu.VMEM((ROWS, 128), BF16),
            pltpu.VMEM((ROWS, 128), F32),
            pltpu.VMEM((64, ROWS), BF16),
            pltpu.VMEM((2, 2 * ROWS, 2 * yl // 8 * 128), BF16),
            pltpu.VMEM((2 * ROWS, 128), F32),
            pltpu.VMEM((ROWS, 128), F32),
            pltpu.VMEM((8, 128), F32),
            pltpu.VMEM((zl, yl, nx), F32),
            pltpu.VMEM((size1, 8, 128), F32),
            pltpu.VMEM((max(size2, 1), 8, 128), F32),
            pltpu.VMEM((8, 128), F32),
            pltpu.VMEM((8, 128), F32),
            pltpu.SemaphoreType.DMA((2, 12)),
            pltpu.SemaphoreType.DMA((2, 12)),
            pltpu.SemaphoreType.DMA((3,)),
            pltpu.SemaphoreType.DMA((size1,)),
            pltpu.SemaphoreType.DMA((size1,)),
            pltpu.SemaphoreType.DMA((size2,)),
            pltpu.SemaphoreType.DMA((size2,)),
        ],
        compiler_params=pltpu.CompilerParams(
            collective_id=0, has_side_effects=True, vmem_limit_bytes=60 * 1024 * 1024
        ),
    )(
        concentration, cotangent, w_in.T, b_in.reshape(1, UNITS), w_out.reshape(1, UNITS), b_out.reshape(1, 1)
    )
    outs = pl.pallas_call(
        hand_over,
        out_shape=(
            jax.ShapeDtypeStruct(concentration.shape, F32),
            jax.ShapeDtypeStruct((4, UNITS), F32),
            jax.ShapeDtypeStruct((1, UNITS), F32),
            jax.ShapeDtypeStruct((1, UNITS), F32),
            jax.ShapeDtypeStruct((1, 1), F32),
        ),
        in_specs=[vmem, vmem],
        out_specs=(vmem, vmem, vmem, vmem, vmem),
    )(*outs)
    return (outs[0], outs[1].T, outs[2].reshape(UNITS), outs[3].reshape(UNITS), outs[4].reshape(()))


def solution(mesh):
    ng, ny = mesh.shape["gz"], mesh.shape["gy"]
    in_specs = (P("gz", "gy", None), P("gz", "gy", None), P(), P(), P(), P())
    out_specs = (P("gz", "gy", None), P(), P(), P(), P())

    def run(*args):
        return per_device(ng, ny, *args)

    return jax.shard_map(run, mesh=mesh, in_specs=in_specs, out_specs=out_specs, check_vma=False)
```

```python
import math

import jax
import jax.numpy as jnp
from jax import lax
from jax.experimental import pallas as pl
from jax.experimental.pallas import tpu as pltpu
from jax.sharding import PartitionSpec as P

KAPPA = 0.5
STEP = 0.008
FLOOR = 0.05
HIGH = lax.Precision.HIGHEST
MESH = pl.DeviceIdType.MESH
F32 = jnp.float32
BF16 = jnp.bfloat16

WC = 7
WA = 4
R = 8
UNITS = 32
ROWS = UNITS * 8


DIRECTIONS = [(dz, dy) for dz in (0, -1, 1) for dy in (-1, 1, 0) if (dz, dy) != (0, 0)]

CORNER_C = ((0, 2, 8), (2, 4, 4))
CORNER_A = ((0, 3, 4),)
PIECES_C = [(dz, dy, n) for dz, dy in DIRECTIONS for n in range(len(CORNER_C) if dz * dy else 1)]
PIECES_A = [(dz, dy, n) for dz, dy in DIRECTIONS for n in range(len(CORNER_A) if dz * dy else 1)]


def iota(shape, dim):
    return lax.broadcasted_iota(jnp.int32, shape, dim)


def xp(v):
    return pltpu.roll(v, v.shape[1] - 1, 1)


def xm(v):
    return pltpu.roll(v, 1, 1)


def yp(v):
    return pltpu.roll(v, v.shape[0] - 1, 0)


def ym(v):
    return pltpu.roll(v, 1, 0)


def split(v):
    high = v.astype(BF16)
    return high, (v - high.astype(F32)).astype(BF16)


def dot(a, b, precision=None):
    return jnp.dot(a, b, preferred_element_type=F32, precision=precision)


def make_kernel(zl, yl, ng, ny, factor):
    nv = yl // 8
    yr = yl + 2 * R
    n_core = 2 if ny % 2 == 0 else 1
    n_z = 8 if ng % 8 == 0 else 1
    size1 = n_core * n_z
    size2 = (ny // n_core) * (ng // n_z)

    def kernel(
        conc, cot, w_in, b_in, w_out, b_out,
        out, out_sums,
        C, A0, MU1, M1, SG1, C2, MU2, M2, SG2, RR, UU, VV, A1, GS, H1, H2,
        WL, WOF, CT, UB, PACC, TACC, GACC, OUTV, RED, RED2, MSG, MSG2,
        send_sem, recv_sem, local_sem, rs_send, rs_recv, rs2_send, rs2_recv,
    ):
        gz = lax.axis_index("gz")
        gy = lax.axis_index("gy")

        def neighbour(dz, dy):
            return (lax.rem(gz + dz + ng, ng), lax.rem(gy + dy + ny, ny))

        place1 = lax.rem(gy, n_core) * n_z + lax.rem(gz, n_z)
        place2 = (gy // n_core) * (ng // n_z) + gz // n_z

        def peer1(k):
            q = lax.rem(place1 + k, size1)
            return q, (gz // n_z * n_z + lax.rem(q, n_z), gy // n_core * n_core + q // n_z)

        def peer2(k):
            q = lax.rem(place2 + k, size2)
            outer = ng // n_z
            return q, (lax.rem(q, outer) * n_z + lax.rem(gz, n_z), q // outer * n_core + lax.rem(gy, n_core))

        local_c = pltpu.make_async_copy(
            conc, C.at[pl.ds(WC, zl), pl.ds(R, yl)], local_sem.at[0])
        local_a = pltpu.make_async_copy(
            cot, A0.at[pl.ds(WA, zl), pl.ds(R, yl)], local_sem.at[1])
        local_c.start()
        local_a.start()

        for margin in (0, R + yl):
            for first, length in ((0, WC - 2), (WC + zl + 2, WC - 2)):
                rows = pl.ds(margin + (0 if margin == 0 else 4), 4)
                C[pl.ds(first, length), rows] = jnp.zeros((length, 4, 128), F32)
            for p in (0, 2 * WC + zl - 1):
                C[p, pl.ds(margin, R)] = jnp.zeros((R, 128), F32)
            rows = pl.ds(margin + (0 if margin == 0 else 4), 4)
            A0[:, rows] = jnp.zeros((zl + 2 * WA, 4, 128), F32)
            for p in (0, 2 * WA + zl - 1):
                A0[p, pl.ds(margin, R)] = jnp.zeros((R, 128), F32)

        barrier = pltpu.get_barrier_semaphore()
        count = 0
        for dz, dy in DIRECTIONS:
            pl.semaphore_signal(barrier, inc=1, device_id=neighbour(dz, dy), device_id_type=MESH)
            count += 1
        for k in range(1, size1):
            pl.semaphore_signal(barrier, inc=1, device_id=peer1(k)[1], device_id_type=MESH)
            count += 1
        for k in range(1, size2):
            pl.semaphore_signal(barrier, inc=1, device_id=peer2(k)[1], device_id_type=MESH)
            count += 1
        pl.semaphore_wait(barrier, count)

        def span(d, size, edge, first, length):
            if d > 0:
                return pl.ds(size - first - length, length), pl.ds(edge - first - length, length)
            if d < 0:
                return pl.ds(first, length), pl.ds(edge + size + first, length)
            return pl.ds(0, size), pl.ds(edge, size)

        def halo(which, source, field, pieces, width, rows, corner):
            copies = {}
            for n, (dz, dy, part) in enumerate(pieces):
                first, planes, high_rows = corner[part] if dz * dy else (0, width, rows)
                sz, tz = span(dz, zl, width, first, planes)
                sy, ty = span(dy, yl, R, 0, high_rows)
                copies[dz, dy, part] = pltpu.make_async_remote_copy(
                    src_ref=source.at[sz, sy],
                    dst_ref=field.at[tz, ty],
                    send_sem=send_sem.at[which, n],
                    recv_sem=recv_sem.at[which, n],
                    device_id=neighbour(dz, dy),
                    device_id_type=MESH,
                )
            return copies

        halo_c = halo(0, conc, C, PIECES_C, WC, 8, CORNER_C)
        halo_a = halo(1, cot, A0, PIECES_A, WA, 4, CORNER_A)
        for dy in (-1, 1):
            halo_c[0, dy, 0].start()

        lane = iota((UNITS, 128), 1)
        eye = iota((UNITS, UNITS), 0) == iota((UNITS, UNITS), 1)
        bi_col = jnp.sum(jnp.where(eye, b_in[...], 0.0), axis=1, keepdims=True)
        wo_col = jnp.sum(jnp.where(eye, w_out[...], 0.0), axis=1, keepdims=True)
        packed = jnp.where(lane == 4, bi_col, jnp.where(lane == 5, wo_col, 0.0))
        for k in range(4):
            w_col = jnp.sum(jnp.where(eye, w_in[k:k + 1, :], 0.0), axis=1, keepdims=True)
            packed = jnp.where(lane == k, w_col, packed)
        spread = (iota((ROWS, UNITS), 0) // 8 == iota((ROWS, UNITS), 1)).astype(F32)
        params = dot(spread, packed, HIGH)
        row = iota((ROWS, 128), 0)
        col = iota((ROWS, 128), 1)
        same = (row & 7) == (col & 7)
        which_k = (col & 31) // 8
        group = col // 32
        w_sel = jnp.zeros((ROWS, 128), F32)
        for k in range(4):
            w_sel = jnp.where(which_k == k, params[:, k:k + 1], w_sel)
        bias = jnp.broadcast_to(params[:, 4:5], (ROWS, 128))
        wo_full = jnp.broadcast_to(params[:, 5:6], (ROWS, 128))
        WOF[...] = wo_full
        value = jnp.where(group == 3, jnp.where(which_k < 2, bias, 0.0), w_sel)
        high = value.astype(BF16).astype(F32)
        low = value - high
        is_low = (group == 1) | ((group == 3) & (which_k == 1))
        WL[...] = jnp.where(same, jnp.where(is_low, low, high), 0.0).astype(BF16)
        joint = w_sel * wo_full
        j_high = joint.astype(BF16).astype(F32)
        j_low = joint - j_high
        j_mat = jnp.where(same, jnp.where(group == 0, j_high, jnp.where(group == 1, j_low, 0.0)), 0.0)
        CT[...] = j_mat.T[0:64].astype(BF16)
        PACC[...] = jnp.zeros((2 * ROWS, 128), F32)
        TACC[...] = jnp.zeros((ROWS, 128), F32)
        GACC[...] = jnp.zeros((8, 128), F32)

        half = iota((8, 128), 0) < 4

        def pack(v):
            blocks = [v[R + 8 * i:R + 8 * i + 8] for i in range(nv)]
            blocks.append(jnp.where(half, v[R + yl:], v[:R]))
            return blocks

        def unpack(blocks):
            return jnp.concatenate([blocks[-1]] + blocks[:-1] + [blocks[-1]], axis=0)

        def fields_of(c_ref, p, rows=slice(None)):
            c = c_ref[p, rows]
            zu, zd = c_ref[p + 1, rows], c_ref[p - 1, rows]
            yu, yd = yp(c), ym(c)
            xu, xd = xp(c), xm(c)
            lap = ((zu + zd) + (yu + yd)) + (xu + xd) - 6.0 * c
            s0, s1, s2 = 0.5 * (zu - zd), 0.5 * (yu - yd), 0.5 * (xu - xd)
            sq = s0 * s0 + s1 * s1 + s2 * s2
            return c, lap, sq, (s0, s1, s2)

        def units(pair):
            feats = jnp.concatenate([jnp.concatenate(f, axis=0) for f in pair], axis=1)
            f_high, f_low = split(feats)
            rhs = jnp.concatenate([f_high, f_high, f_low, jnp.ones((32, 256), BF16)], axis=0)
            return jnp.tanh(dot(WL[...], rhs))

        def score(h):
            wo = WOF[...]
            weighted = h * jnp.concatenate([wo, wo], axis=1)
            return jnp.sum(weighted.reshape(UNITS, 8, 256), axis=0) + b_out[0, 0]

        def soft(s):
            e = jnp.exp(s)
            return jnp.log(1.0 + e) + FLOOR, e / (1.0 + e)

        def forward_blocks(q, feats, ids, offset):
            pair = [[f[8 * i - offset:8 * i - offset + 8] for f in feats] for i in ids]
            h = units(pair)
            if ids[0] > nv:
                mask = (iota((ROWS, 128), 0) & 7) < 4
                H1[q, nv] = jnp.where(mask, h[:, :128], h[:, 128:])
            else:
                for i in range(2):
                    H1[q, ids[i] - 1] = h[:, 128 * i:128 * i + 128]
            m, sg = soft(score(h))
            for i in range(2):
                rows = pl.ds(8 * ids[i], 8)
                M1[q, rows] = m[:, 128 * i:128 * i + 128]
                SG1[q, rows] = sg[:, 128 * i:128 * i + 128]

        def forward_one_early(planes):
            for q in planes:
                c, lap, sq, _ = fields_of(C, q, pl.ds(R, yl))
                feats = [c, lap, sq, c * c * c - c - KAPPA * lap]
                for i in range(2, nv, 2):
                    forward_blocks(q, feats, (i, i + 1), R)

        def forward_one(planes, early=False):
            for q in planes:
                c, lap, sq, _ = fields_of(C, q)
                mu = c * c * c - c - KAPPA * lap
                MU1[q] = mu
                feats = [c, lap, sq, mu]
                if not early:
                    for i in range(2, nv, 2):
                        forward_blocks(q, feats, (i, i + 1), 0)
                forward_blocks(q, feats, (1, nv), 0)
                forward_blocks(q, feats, (nv + 1, 0), 0)

        def wait_for(copies, sides):
            for dz, dy, part in copies:
                if (dz == 0) == (sides == "y"):
                    copies[dz, dy, part].wait_recv()

        low, high = WC, WC + zl - 1

        def inner(width, body):
            for p in range(low + width, high - width, 2):
                body((p, p + 1))

        def outer(first, last, body):
            for k in range(-first, last):
                body((low - 1 - k, high + 1 + k))

        def advance(planes):
            for p in planes:
                advance_plane(p)

        def advance_plane(p):
            mu, m = MU1[p], M1[p]
            def face(mu_a, m_a, mu_b, m_b):
                return (m_a + m_b) * (mu_b - mu_a)
            up = face(mu, m, MU1[p + 1], M1[p + 1])
            down = face(MU1[p - 1], M1[p - 1], mu, m)
            fy = face(mu, m, yp(mu), yp(m))
            fx = face(mu, m, xp(mu), xp(m))
            total = (up - down) + (fy - ym(fy)) + (fx - xm(fx))
            C2[p] = C[p] + (0.5 * STEP) * total

        def forward_two(planes):
            feats = []
            for q in planes:
                c, lap, sq, _ = fields_of(C2, q)
                mu = c * c * c - c - KAPPA * lap
                MU2[q] = mu
                feats.append([pack(f) for f in (c, lap, sq, mu)])
            work = [((d, a), (d, a + 1)) for d in range(2) for a in range(0, nv, 2)] + [((0, nv), (1, nv))]
            for places in work:
                h = units([[f[a] for f in feats[d]] for d, a in places])
                m, sg = soft(score(h))
                for i, (d, a) in enumerate(places):
                    q = planes[d]
                    H2[q, a] = h[:, 128 * i:128 * i + 128]
                    mi, si = m[:, 128 * i:128 * i + 128], sg[:, 128 * i:128 * i + 128]
                    for start in ([R + 8 * a] if a < nv else [0, R + yl]):
                        M2[q, pl.ds(start, 8)] = mi
                        SG2[q, pl.ds(start, 8)] = si

        def jumps(q, adj, shift):
            a = adj[q + shift]
            return adj[q + 1 + shift] - a, a - adj[q - 1 + shift], yp(a) - a, xp(a) - a

        def faces(field, q, da, of):
            v = field[q]
            up = of(v, field[q + 1], da[0])
            down = of(field[q - 1], v, da[1])
            fy = of(v, yp(v), da[2])
            fx = of(v, xp(v), da[3])
            return (up, down), (fy, ym(fy)), (fx, xm(fx))

        def score_adjoint(q, da, mu_ref, sg_ref):
            z, y, x = faces(mu_ref, q, da, lambda here, there, d: (there - here) * d)
            adj_mob = (z[0] + z[1]) + (y[0] + y[1]) + (x[0] + x[1])
            return (-0.5 * STEP) * adj_mob * sg_ref[q]

        def flux_adjoint(q, da, m_ref):
            z, y, x = faces(m_ref, q, da, lambda here, there, d: (here + there) * d)
            return (0.5 * STEP) * ((z[0] - z[1]) + (y[0] - y[1]) + (x[0] - x[1]))

        def places_of(with_core, with_sides):
            core = [((d, b), (d, b + 1)) for d in range(2) for b in range(0, nv, 2)] if with_core else []
            return core + ([((0, nv), (1, nv))] if with_sides else [])

        def hidden(planes, places, h_ref):
            h = jnp.concatenate([h_ref[planes[d], b] for d, b in places], axis=1)
            return 1.0 - h * h

        def sums(planes, g, local, mu_ref, h_ref, ub):
            feats = []
            for q, (c, lap, sq, _) in zip(planes, local):
                feats.append([pack(f) for f in (c, lap, sq, mu_ref[q])])
            gg = []
            for n, places in enumerate(places_of(True, False)):
                u = hidden(planes, places, h_ref)
                u_high, u_low = split(u)
                ub[pl.ds(0, ROWS), pl.ds(256 * n, 256)] = u_high
                ub[pl.ds(ROWS, ROWS), pl.ds(256 * n, 256)] = u_low
                gs = jnp.concatenate([g[d][b] for d, b in places], axis=1)
                stack = [gs * jnp.concatenate([feats[d][k][b] for d, b in places], axis=1) for k in range(4)]
                s_high, s_low = split(jnp.concatenate(stack + [gs, jnp.zeros((8, 256), F32)], axis=0))
                gg.append(jnp.concatenate([s_high, s_low, jnp.zeros((32, 256), BF16)], axis=0))
            PACC[...] += lax.dot_general(
                ub[...], jnp.concatenate(gg, axis=1), (((1,), (1,)), ((), ())), preferred_element_type=F32)
            total = TACC[...].reshape(UNITS, 8, 128)
            g_total = GACC[...]
            for d in range(2):
                for b in range(nv):
                    total = total + h_ref[planes[d], b].reshape(UNITS, 8, 128) * g[d][b][None]
                    g_total = g_total + g[d][b]
            TACC[...] = total.reshape(ROWS, 128)
            GACC[...] = g_total

        def finish(planes, g, steps, local, adj, shift, m_ref, h_ref, ub=None):
            A = [[None] * (nv + 1) for _ in planes]
            for n, places in enumerate(places_of(True, True)):
                if ub is not None and n < nv:
                    u_high = ub[pl.ds(0, ROWS), pl.ds(256 * n, 256)]
                else:
                    u_high = hidden(planes, places, h_ref).astype(BF16)
                back = dot(CT[...], u_high)
                back = back[:32] + back[32:]
                for i, (d, b) in enumerate(places):
                    A[d][b] = [back[8 * k:8 * k + 8, 128 * i:128 * i + 128] * g[d][b] for k in range(4)]
            for d, q in enumerate(planes):
                a_c, a_lap, a_sq, a_mu = (unpack([A[d][b][k] for b in range(nv + 1)]) for k in range(4))
                c, _, _, slopes = local[d]
                adj_pot = flux_adjoint(q, steps[d], m_ref) + a_mu
                adj_lap = a_lap - KAPPA * adj_pot
                zed, why, ex = (a_sq * slope for slope in slopes)
                rest = adj[q + shift] + a_c + (3.0 * c * c - 1.0) * adj_pot - 6.0 * adj_lap
                rest = rest + (xm(adj_lap + ex) + xp(adj_lap - ex)) + (ym(adj_lap + why) + yp(adj_lap - why))
                RR[q] = rest
                UU[q] = adj_lap + zed
                VV[q] = adj_lap - zed

        turn = [0]

        def buffer():
            turn[0] ^= 1
            return UB.at[turn[0]]

        def start_of(planes, adj, shift, c_ref):
            return [jumps(q, adj, shift) for q in planes], [fields_of(c_ref, q) for q in planes]

        def back_two(with_sums):
            def body(planes):
                shift = WA - WC
                steps, local = start_of(planes, A0, shift, C2)
                g = [pack(score_adjoint(q, da, MU2, SG2)) for q, da in zip(planes, steps)]
                ub = buffer() if with_sums else None
                if with_sums:
                    sums(planes, g, local, MU2, H2, ub)
                finish(planes, g, steps, local, A0, shift, M2, H2, ub)
            return body

        def back_one_sums(planes):
            steps, local = start_of(planes, A1, 0, C)
            g = [pack(score_adjoint(q, da, MU1, SG1)) for q, da in zip(planes, steps)]
            sums(planes, g, local, MU1, H1, buffer())
            for d, q in enumerate(planes):
                for b in range(nv + 1):
                    GS[q, pl.ds(8 * b, 8)] = g[d][b]

        def back_one_rest(planes):
            steps, local = start_of(planes, A1, 0, C)
            g = [[GS[q, pl.ds(8 * b, 8)] for b in range(nv + 1)] for q in planes]
            finish(planes, g, steps, local, A1, 0, M1, H1)

        def back_one_sides(planes):
            steps, local = start_of(planes, A1, 0, C)
            g = [pack(score_adjoint(q, da, MU1, SG1)) for q, da in zip(planes, steps)]
            finish(planes, g, steps, local, A1, 0, M1, H1)

        def join(p):
            A1[p] = RR[p] + UU[p - 1] + VV[p + 1]

        for dz, dy, part in PIECES_C:
            if dz != 0:
                halo_c[dz, dy, part].start()
        local_c.wait()
        inner(1, forward_one_early)
        wait_for(halo_c, "y")
        for dy in (-1, 1):
            halo_a[0, dy, 0].start()
        inner(1, lambda planes: forward_one(planes, True))
        inner(2, advance)
        inner(3, forward_two)
        local_a.wait()
        wait_for(halo_a, "y")
        for dz, dy, _ in PIECES_A:
            if dz != 0:
                halo_a[dz, dy, 0].start()
        inner(4, back_two(True))
        for p in range(low + 5, high - 4):
            join(p)
        inner(6, back_one_sums)
        wait_for(halo_c, "z")
        outer(1, 6, forward_one)
        outer(2, 5, advance)
        outer(3, 4, forward_two)
        wait_for(halo_a, "z")
        outer(4, 0, back_two(True))
        outer(0, 3, back_two(False))
        for p in [*range(low - 2, low + 5), *range(high - 4, high + 3)]:
            join(p)
        outer(6, 0, back_one_sums)

        both = PACC[pl.ds(0, ROWS)] + PACC[pl.ds(ROWS, ROWS)]
        both = jnp.where(same & (col < 96), both, 0.0)
        gather = (iota((UNITS, ROWS), 1) // 8 == iota((UNITS, ROWS), 0)).astype(F32)
        by_unit = dot(gather, both, HIGH)
        c_row = iota((128, 128), 0)
        c_col = iota((128, 128), 1)
        c_k = jnp.where(c_row < 48, c_row, c_row - 48) // 8
        collect = ((c_k == c_col) & (c_row < 96) & (c_col < 5)).astype(F32)
        grads = dot(by_unit, collect, HIGH) * wo_col
        t_col = jnp.sum(dot(gather, TACC[...], HIGH), axis=1, keepdims=True)
        g_sum = jnp.sum(jnp.sum(GACC[...], axis=0, keepdims=True), axis=1, keepdims=True)
        first_row = iota((UNITS, 128), 0) == 0
        grads = jnp.where(lane == 5, t_col, grads)
        grads = jnp.where((lane == 6) & first_row, g_sum, grads)
        square = jnp.concatenate([grads, jnp.zeros((128 - UNITS, 128), F32)], axis=0)
        MSG[...] = square.T[0:8]

        def exchange(size, place, peer, src, slots, s_sem, r_sem):
            copies = []
            for k in range(1, size):
                q, device = peer(k)
                copy = pltpu.make_async_remote_copy(
                    src_ref=src, dst_ref=slots.at[place], send_sem=s_sem.at[k],
                    recv_sem=r_sem.at[place], device_id=device, device_id_type=MESH)
                copy.start()
                copies.append(copy)
            slots[place] = src[...]
            return copies

        def collected(size, peer, copies, src, slots, s_sem, r_sem):
            for k in range(1, size):
                q, device = peer(k)
                pltpu.make_async_remote_copy(
                    src_ref=src, dst_ref=slots.at[q], send_sem=s_sem.at[k],
                    recv_sem=r_sem.at[q], device_id=device, device_id_type=MESH).wait_recv()
            total = slots[0]
            for k in range(1, size):
                total = total + slots[k]
            return total

        sent1 = exchange(size1, place1, peer1, MSG, RED, rs_send, rs_recv)

        outer(0, 1, back_one_sides)
        inner(4, back_one_rest)
        total = collected(size1, peer1, sent1, MSG, RED, rs_send, rs_recv)
        MSG2[...] = total
        sent2 = exchange(size2, place2, peer2, MSG2, RED2, rs2_send, rs2_recv)
        outer(4, 0, back_one_rest)
        for p in range(low, high + 1):
            rows = pl.ds(R, yl)
            OUTV[p - WC] = RR[p, rows] + UU[p - 1, rows] + VV[p + 1, rows]
        write = pltpu.make_async_copy(OUTV, out, local_sem.at[2])
        write.start()

        total = collected(size2, peer2, sent2, MSG2, RED2, rs2_send, rs2_recv)
        out_sums[...] = total * factor

        for copy in [*halo_c.values(), *halo_a.values(), *sent1, *sent2]:
            copy.wait_send()
        write.wait()

    return kernel, yr, size1, size2


def hand_over(field, sums, out, out_wi, out_bi, out_wo, out_bo):
    out[...] = field[...]
    out_wi[...] = sums[0:4, 0:UNITS]
    out_bi[...] = sums[4:5, 0:UNITS]
    out_wo[...] = sums[5:6, 0:UNITS]
    out_bo[...] = sums[6:7, 0:1]


def per_device(ng, ny, concentration, cotangent, w_in, b_in, w_out, b_out):
    zl, yl, nx = concentration.shape
    factor = 1.0 / (STEP * math.sqrt(float(zl * yl * nx * ng * ny)))
    kernel, yr, size1, size2 = make_kernel(zl, yl, ng, ny, factor)
    planes = zl + 2 * WC
    nv = yl // 8
    field = pltpu.VMEM((planes, yr, nx), F32)
    anywhere = pl.BlockSpec(memory_space=pl.ANY)
    vmem = pl.BlockSpec(memory_space=pltpu.VMEM)
    smem = pl.BlockSpec(memory_space=pltpu.SMEM)
    outs = pl.pallas_call(
        kernel,
        out_shape=(
            jax.ShapeDtypeStruct(concentration.shape, F32),
            jax.ShapeDtypeStruct((8, 128), F32),
        ),
        in_specs=[anywhere, anywhere, vmem, vmem, vmem, smem],
        out_specs=(anywhere, vmem),
        scratch_shapes=[
            field,
            pltpu.VMEM((zl + 2 * WA, yr, nx), F32),
            field, field, field,
            field, field, field, field,
            field, field, field, field,
            pltpu.VMEM((planes, yl + 8, nx), F32),
            pltpu.VMEM((planes, nv + 1, ROWS, nx), F32),
            pltpu.VMEM((planes, nv + 1, ROWS, nx), F32),
            pltpu.VMEM((ROWS, 128), BF16),
            pltpu.VMEM((ROWS, 128), F32),
            pltpu.VMEM((64, ROWS), BF16),
            pltpu.VMEM((2, 2 * ROWS, 2 * yl // 8 * 128), BF16),
            pltpu.VMEM((2 * ROWS, 128), F32),
            pltpu.VMEM((ROWS, 128), F32),
            pltpu.VMEM((8, 128), F32),
            pltpu.VMEM((zl, yl, nx), F32),
            pltpu.VMEM((size1, 8, 128), F32),
            pltpu.VMEM((max(size2, 1), 8, 128), F32),
            pltpu.VMEM((8, 128), F32),
            pltpu.VMEM((8, 128), F32),
            pltpu.SemaphoreType.DMA((2, 12)),
            pltpu.SemaphoreType.DMA((2, 12)),
            pltpu.SemaphoreType.DMA((3,)),
            pltpu.SemaphoreType.DMA((size1,)),
            pltpu.SemaphoreType.DMA((size1,)),
            pltpu.SemaphoreType.DMA((size2,)),
            pltpu.SemaphoreType.DMA((size2,)),
        ],
        compiler_params=pltpu.CompilerParams(
            collective_id=0, has_side_effects=True, vmem_limit_bytes=60 * 1024 * 1024
        ),
    )(
        concentration, cotangent, w_in.T, b_in.reshape(1, UNITS), w_out.reshape(1, UNITS), b_out.reshape(1, 1)
    )
    outs = pl.pallas_call(
        hand_over,
        out_shape=(
            jax.ShapeDtypeStruct(concentration.shape, F32),
            jax.ShapeDtypeStruct((4, UNITS), F32),
            jax.ShapeDtypeStruct((1, UNITS), F32),
            jax.ShapeDtypeStruct((1, UNITS), F32),
            jax.ShapeDtypeStruct((1, 1), F32),
        ),
        in_specs=[vmem, vmem],
        out_specs=(vmem, vmem, vmem, vmem, vmem),
    )(*outs)
    return (outs[0], outs[1].T, outs[2].reshape(UNITS), outs[3].reshape(UNITS), outs[4].reshape(()))


def solution(mesh):
    ng, ny = mesh.shape["gz"], mesh.shape["gy"]
    in_specs = (P("gz", "gy", None), P("gz", "gy", None), P(), P(), P(), P())
    out_specs = (P("gz", "gy", None), P(), P(), P(), P())

    def run(*args):
        return per_device(ng, ny, *args)

    return jax.shard_map(run, mesh=mesh, in_specs=in_specs, out_specs=out_specs, check_vma=False)
```

```python
import math

import jax
import jax.numpy as jnp
from jax import lax
from jax.experimental import pallas as pl
from jax.experimental.pallas import tpu as pltpu
from jax.sharding import PartitionSpec as P

KAPPA = 0.5
STEP = 0.008
FLOOR = 0.05
HIGH = lax.Precision.HIGHEST
MESH = pl.DeviceIdType.MESH
F32 = jnp.float32
BF16 = jnp.bfloat16

WC = 7
WA = 4
R = 8
UNITS = 32
ROWS = UNITS * 8


DIRECTIONS = [(dz, dy) for dz in (0, -1, 1) for dy in (-1, 1, 0) if (dz, dy) != (0, 0)]

CORNER_C = ((0, 2, 8), (2, 4, 4))
CORNER_A = ((0, 3, 4),)
PIECES_C = [(dz, dy, n) for dz, dy in DIRECTIONS for n in range(len(CORNER_C) if dz * dy else 1)]
PIECES_A = [(dz, dy, n) for dz, dy in DIRECTIONS for n in range(len(CORNER_A) if dz * dy else 1)]


def iota(shape, dim):
    return lax.broadcasted_iota(jnp.int32, shape, dim)


def xp(v):
    return pltpu.roll(v, v.shape[1] - 1, 1)


def xm(v):
    return pltpu.roll(v, 1, 1)


def yp(v):
    return pltpu.roll(v, v.shape[0] - 1, 0)


def ym(v):
    return pltpu.roll(v, 1, 0)


def split(v):
    high = v.astype(BF16)
    return high, (v - high.astype(F32)).astype(BF16)


def dot(a, b, precision=None):
    return jnp.dot(a, b, preferred_element_type=F32, precision=precision)


def make_kernel(zl, yl, ng, ny, factor):
    nv = yl // 8
    yr = yl + 2 * R
    n_core = 2 if ny % 2 == 0 else 1
    n_z = 8 if ng % 8 == 0 else 1
    size1 = n_core * n_z
    size2 = (ny // n_core) * (ng // n_z)

    def kernel(
        conc, cot, w_in, b_in, w_out, b_out,
        out, out_sums,
        C, A0, MU1, M1, SG1, C2, MU2, M2, SG2, RR, UU, VV, A1, GS, H1, H2,
        WL, WOF, CT, UB, PACC, TACC, GACC, OUTV, RED, RED2, MSG, MSG2,
        send_sem, recv_sem, local_sem, rs_send, rs_recv, rs2_send, rs2_recv,
    ):
        gz = lax.axis_index("gz")
        gy = lax.axis_index("gy")

        def neighbour(dz, dy):
            return (lax.rem(gz + dz + ng, ng), lax.rem(gy + dy + ny, ny))

        place1 = lax.rem(gy, n_core) * n_z + lax.rem(gz, n_z)
        place2 = (gy // n_core) * (ng // n_z) + gz // n_z

        def peer1(k):
            q = lax.rem(place1 + k, size1)
            return q, (gz // n_z * n_z + lax.rem(q, n_z), gy // n_core * n_core + q // n_z)

        def peer2(k):
            q = lax.rem(place2 + k, size2)
            outer = ng // n_z
            return q, (lax.rem(q, outer) * n_z + lax.rem(gz, n_z), q // outer * n_core + lax.rem(gy, n_core))

        local_c = pltpu.make_async_copy(
            conc, C.at[pl.ds(WC, zl), pl.ds(R, yl)], local_sem.at[0])
        local_a = pltpu.make_async_copy(
            cot, A0.at[pl.ds(WA, zl), pl.ds(R, yl)], local_sem.at[1])
        local_c.start()
        local_a.start()

        for margin in (0, R + yl):
            for first, length in ((0, WC - 2), (WC + zl + 2, WC - 2)):
                rows = pl.ds(margin + (0 if margin == 0 else 4), 4)
                C[pl.ds(first, length), rows] = jnp.zeros((length, 4, 128), F32)
            for p in (0, 2 * WC + zl - 1):
                C[p, pl.ds(margin, R)] = jnp.zeros((R, 128), F32)
            rows = pl.ds(margin + (0 if margin == 0 else 4), 4)
            A0[:, rows] = jnp.zeros((zl + 2 * WA, 4, 128), F32)
            for p in (0, 2 * WA + zl - 1):
                A0[p, pl.ds(margin, R)] = jnp.zeros((R, 128), F32)

        barrier = pltpu.get_barrier_semaphore()
        count = 0
        for dz, dy in DIRECTIONS:
            pl.semaphore_signal(barrier, inc=1, device_id=neighbour(dz, dy), device_id_type=MESH)
            count += 1
        for k in range(1, size1):
            pl.semaphore_signal(barrier, inc=1, device_id=peer1(k)[1], device_id_type=MESH)
            count += 1
        for k in range(1, size2):
            pl.semaphore_signal(barrier, inc=1, device_id=peer2(k)[1], device_id_type=MESH)
            count += 1
        pl.semaphore_wait(barrier, count)

        def span(d, size, edge, first, length):
            if d > 0:
                return pl.ds(size - first - length, length), pl.ds(edge - first - length, length)
            if d < 0:
                return pl.ds(first, length), pl.ds(edge + size + first, length)
            return pl.ds(0, size), pl.ds(edge, size)

        def halo(which, source, field, pieces, width, rows, corner):
            copies = {}
            for n, (dz, dy, part) in enumerate(pieces):
                first, planes, high_rows = corner[part] if dz * dy else (0, width, rows)
                sz, tz = span(dz, zl, width, first, planes)
                sy, ty = span(dy, yl, R, 0, high_rows)
                copies[dz, dy, part] = pltpu.make_async_remote_copy(
                    src_ref=source.at[sz, sy],
                    dst_ref=field.at[tz, ty],
                    send_sem=send_sem.at[which, n],
                    recv_sem=recv_sem.at[which, n],
                    device_id=neighbour(dz, dy),
                    device_id_type=MESH,
                )
            return copies

        halo_c = halo(0, conc, C, PIECES_C, WC, 8, CORNER_C)
        halo_a = halo(1, cot, A0, PIECES_A, WA, 4, CORNER_A)
        for dy in (-1, 1):
            halo_c[0, dy, 0].start()

        lane = iota((UNITS, 128), 1)
        eye = iota((UNITS, UNITS), 0) == iota((UNITS, UNITS), 1)
        bi_col = jnp.sum(jnp.where(eye, b_in[...], 0.0), axis=1, keepdims=True)
        wo_col = jnp.sum(jnp.where(eye, w_out[...], 0.0), axis=1, keepdims=True)
        packed = jnp.where(lane == 4, bi_col, jnp.where(lane == 5, wo_col, 0.0))
        for k in range(4):
            w_col = jnp.sum(jnp.where(eye, w_in[k:k + 1, :], 0.0), axis=1, keepdims=True)
            packed = jnp.where(lane == k, w_col, packed)
        spread = (iota((ROWS, UNITS), 0) // 8 == iota((ROWS, UNITS), 1)).astype(F32)
        params = dot(spread, packed, HIGH)
        row = iota((ROWS, 128), 0)
        col = iota((ROWS, 128), 1)
        same = (row & 7) == (col & 7)
        which_k = (col & 31) // 8
        group = col // 32
        w_sel = jnp.zeros((ROWS, 128), F32)
        for k in range(4):
            w_sel = jnp.where(which_k == k, params[:, k:k + 1], w_sel)
        bias = jnp.broadcast_to(params[:, 4:5], (ROWS, 128))
        wo_full = jnp.broadcast_to(params[:, 5:6], (ROWS, 128))
        WOF[...] = wo_full
        value = jnp.where(group == 3, jnp.where(which_k < 2, bias, 0.0), w_sel)
        high = value.astype(BF16).astype(F32)
        low = value - high
        is_low = (group == 1) | ((group == 3) & (which_k == 1))
        WL[...] = jnp.where(same, jnp.where(is_low, low, high), 0.0).astype(BF16)
        joint = w_sel * wo_full
        j_high = joint.astype(BF16).astype(F32)
        j_low = joint - j_high
        j_mat = jnp.where(same, jnp.where(group == 0, j_high, jnp.where(group == 1, j_low, 0.0)), 0.0)
        CT[...] = j_mat.T[0:64].astype(BF16)
        PACC[...] = jnp.zeros((2 * ROWS, 128), F32)
        TACC[...] = jnp.zeros((ROWS, 128), F32)
        GACC[...] = jnp.zeros((8, 128), F32)

        half = iota((8, 128), 0) < 4

        def pack(v):
            blocks = [v[R + 8 * i:R + 8 * i + 8] for i in range(nv)]
            blocks.append(jnp.where(half, v[R + yl:], v[:R]))
            return blocks

        def unpack(blocks):
            return jnp.concatenate([blocks[-1]] + blocks[:-1] + [blocks[-1]], axis=0)

        def fields_of(c_ref, p, rows=slice(None)):
            c = c_ref[p, rows]
            zu, zd = c_ref[p + 1, rows], c_ref[p - 1, rows]
            yu, yd = yp(c), ym(c)
            xu, xd = xp(c), xm(c)
            lap = ((zu + zd) + (yu + yd)) + (xu + xd) - 6.0 * c
            s0, s1, s2 = 0.5 * (zu - zd), 0.5 * (yu - yd), 0.5 * (xu - xd)
            sq = s0 * s0 + s1 * s1 + s2 * s2
            return c, lap, sq, (s0, s1, s2)

        def units(pair):
            feats = jnp.concatenate([jnp.concatenate(f, axis=0) for f in pair], axis=1)
            f_high, f_low = split(feats)
            rhs = jnp.concatenate([f_high, f_high, f_low, jnp.ones((32, 256), BF16)], axis=0)
            return jnp.tanh(dot(WL[...], rhs))

        def score(h):
            wo = WOF[...]
            weighted = h * jnp.concatenate([wo, wo], axis=1)
            return jnp.sum(weighted.reshape(UNITS, 8, 256), axis=0) + b_out[0, 0]

        def soft(s):
            e = jnp.exp(s)
            return jnp.log(1.0 + e) + FLOOR, e / (1.0 + e)

        def forward_blocks(q, feats, ids, offset):
            pair = [[f[8 * i - offset:8 * i - offset + 8] for f in feats] for i in ids]
            h = units(pair)
            if ids[0] > nv:
                mask = (iota((ROWS, 128), 0) & 7) < 4
                H1[q, nv] = jnp.where(mask, h[:, :128], h[:, 128:])
            else:
                for i in range(2):
                    H1[q, ids[i] - 1] = h[:, 128 * i:128 * i + 128]
            m, sg = soft(score(h))
            for i in range(2):
                rows = pl.ds(8 * ids[i], 8)
                M1[q, rows] = m[:, 128 * i:128 * i + 128]
                SG1[q, rows] = sg[:, 128 * i:128 * i + 128]

        def forward_one_early(planes):
            for q in planes:
                c, lap, sq, _ = fields_of(C, q, pl.ds(R, yl))
                feats = [c, lap, sq, c * c * c - c - KAPPA * lap]
                for i in range(2, nv, 2):
                    forward_blocks(q, feats, (i, i + 1), R)

        def forward_one(planes, early=False):
            for q in planes:
                c, lap, sq, _ = fields_of(C, q)
                mu = c * c * c - c - KAPPA * lap
                MU1[q] = mu
                feats = [c, lap, sq, mu]
                if not early:
                    for i in range(2, nv, 2):
                        forward_blocks(q, feats, (i, i + 1), 0)
                forward_blocks(q, feats, (1, nv), 0)
                forward_blocks(q, feats, (nv + 1, 0), 0)

        def wait_for(copies, sides):
            for dz, dy, part in copies:
                if (dz == 0) == (sides == "y"):
                    copies[dz, dy, part].wait_recv()

        low, high = WC, WC + zl - 1

        def inner(width, body):
            for p in range(low + width, high - width, 2):
                body((p, p + 1))

        def outer(first, last, body):
            for k in range(-first, last):
                body((low - 1 - k, high + 1 + k))

        def advance(planes):
            for p in planes:
                advance_plane(p)

        def advance_plane(p):
            mu, m = MU1[p], M1[p]
            def face(mu_a, m_a, mu_b, m_b):
                return (m_a + m_b) * (mu_b - mu_a)
            up = face(mu, m, MU1[p + 1], M1[p + 1])
            down = face(MU1[p - 1], M1[p - 1], mu, m)
            fy = face(mu, m, yp(mu), yp(m))
            fx = face(mu, m, xp(mu), xp(m))
            total = (up - down) + (fy - ym(fy)) + (fx - xm(fx))
            C2[p] = C[p] + (0.5 * STEP) * total

        def forward_two(planes):
            feats = []
            for q in planes:
                c, lap, sq, _ = fields_of(C2, q)
                mu = c * c * c - c - KAPPA * lap
                MU2[q] = mu
                feats.append([pack(f) for f in (c, lap, sq, mu)])
            work = [((d, a), (d, a + 1)) for d in range(2) for a in range(0, nv, 2)] + [((0, nv), (1, nv))]
            for places in work:
                h = units([[f[a] for f in feats[d]] for d, a in places])
                m, sg = soft(score(h))
                for i, (d, a) in enumerate(places):
                    q = planes[d]
                    H2[q, a] = h[:, 128 * i:128 * i + 128]
                    mi, si = m[:, 128 * i:128 * i + 128], sg[:, 128 * i:128 * i + 128]
                    for start in ([R + 8 * a] if a < nv else [0, R + yl]):
                        M2[q, pl.ds(start, 8)] = mi
                        SG2[q, pl.ds(start, 8)] = si

        def jumps(q, adj, shift):
            a = adj[q + shift]
            return adj[q + 1 + shift] - a, a - adj[q - 1 + shift], yp(a) - a, xp(a) - a

        def faces(field, q, da, of):
            v = field[q]
            up = of(v, field[q + 1], da[0])
            down = of(field[q - 1], v, da[1])
            fy = of(v, yp(v), da[2])
            fx = of(v, xp(v), da[3])
            return (up, down), (fy, ym(fy)), (fx, xm(fx))

        def score_adjoint(q, da, mu_ref, sg_ref):
            z, y, x = faces(mu_ref, q, da, lambda here, there, d: (there - here) * d)
            adj_mob = (z[0] + z[1]) + (y[0] + y[1]) + (x[0] + x[1])
            return (-0.5 * STEP) * adj_mob * sg_ref[q]

        def flux_adjoint(q, da, m_ref):
            z, y, x = faces(m_ref, q, da, lambda here, there, d: (here + there) * d)
            return (0.5 * STEP) * ((z[0] - z[1]) + (y[0] - y[1]) + (x[0] - x[1]))

        def places_of(with_core, with_sides):
            core = [((d, b), (d, b + 1)) for d in range(2) for b in range(0, nv, 2)] if with_core else []
            return core + ([((0, nv), (1, nv))] if with_sides else [])

        def hidden(planes, places, h_ref):
            h = jnp.concatenate([h_ref[planes[d], b] for d, b in places], axis=1)
            return 1.0 - h * h

        def sums(planes, g, local, mu_ref, h_ref, ub):
            feats = []
            for q, (c, lap, sq, _) in zip(planes, local):
                feats.append([pack(f) for f in (c, lap, sq, mu_ref[q])])
            gg = []
            for n, places in enumerate(places_of(True, False)):
                u = hidden(planes, places, h_ref)
                u_high, u_low = split(u)
                ub[pl.ds(0, ROWS), pl.ds(256 * n, 256)] = u_high
                ub[pl.ds(ROWS, ROWS), pl.ds(256 * n, 256)] = u_low
                gs = jnp.concatenate([g[d][b] for d, b in places], axis=1)
                stack = [gs * jnp.concatenate([feats[d][k][b] for d, b in places], axis=1) for k in range(4)]
                s_high, s_low = split(jnp.concatenate(stack + [gs, jnp.zeros((8, 256), F32)], axis=0))
                gg.append(jnp.concatenate([s_high, s_low, jnp.zeros((32, 256), BF16)], axis=0))
            PACC[...] += lax.dot_general(
                ub[...], jnp.concatenate(gg, axis=1), (((1,), (1,)), ((), ())), preferred_element_type=F32)
            total = TACC[...].reshape(UNITS, 8, 128)
            g_total = GACC[...]
            for d in range(2):
                for b in range(nv):
                    total = total + h_ref[planes[d], b].reshape(UNITS, 8, 128) * g[d][b][None]
                    g_total = g_total + g[d][b]
            TACC[...] = total.reshape(ROWS, 128)
            GACC[...] = g_total

        def finish(planes, g, steps, local, adj, shift, m_ref, h_ref, ub=None):
            A = [[None] * (nv + 1) for _ in planes]
            for n, places in enumerate(places_of(True, True)):
                if ub is not None and n < nv:
                    u_high = ub[pl.ds(0, ROWS), pl.ds(256 * n, 256)]
                else:
                    u_high = hidden(planes, places, h_ref).astype(BF16)
                back = dot(CT[...], u_high)
                back = back[:32] + back[32:]
                for i, (d, b) in enumerate(places):
                    A[d][b] = [back[8 * k:8 * k + 8, 128 * i:128 * i + 128] * g[d][b] for k in range(4)]
            for d, q in enumerate(planes):
                a_c, a_lap, a_sq, a_mu = (unpack([A[d][b][k] for b in range(nv + 1)]) for k in range(4))
                c, _, _, slopes = local[d]
                adj_pot = flux_adjoint(q, steps[d], m_ref) + a_mu
                adj_lap = a_lap - KAPPA * adj_pot
                zed, why, ex = (a_sq * slope for slope in slopes)
                rest = adj[q + shift] + a_c + (3.0 * c * c - 1.0) * adj_pot - 6.0 * adj_lap
                rest = rest + (xm(adj_lap + ex) + xp(adj_lap - ex)) + (ym(adj_lap + why) + yp(adj_lap - why))
                RR[q] = rest
                UU[q] = adj_lap + zed
                VV[q] = adj_lap - zed

        turn = [0]

        def buffer():
            turn[0] ^= 1
            return UB.at[turn[0]]

        def start_of(planes, adj, shift, c_ref):
            return [jumps(q, adj, shift) for q in planes], [fields_of(c_ref, q) for q in planes]

        def back_two(with_sums):
            def body(planes):
                shift = WA - WC
                steps, local = start_of(planes, A0, shift, C2)
                g = [pack(score_adjoint(q, da, MU2, SG2)) for q, da in zip(planes, steps)]
                ub = buffer() if with_sums else None
                if with_sums:
                    sums(planes, g, local, MU2, H2, ub)
                finish(planes, g, steps, local, A0, shift, M2, H2, ub)
            return body

        def back_one_sums(planes):
            steps, local = start_of(planes, A1, 0, C)
            g = [pack(score_adjoint(q, da, MU1, SG1)) for q, da in zip(planes, steps)]
            sums(planes, g, local, MU1, H1, buffer())
            for d, q in enumerate(planes):
                for b in range(nv + 1):
                    GS[q, pl.ds(8 * b, 8)] = g[d][b]

        def back_one_rest(planes):
            steps, local = start_of(planes, A1, 0, C)
            g = [[GS[q, pl.ds(8 * b, 8)] for b in range(nv + 1)] for q in planes]
            finish(planes, g, steps, local, A1, 0, M1, H1)

        def back_one_sides(planes):
            steps, local = start_of(planes, A1, 0, C)
            g = [pack(score_adjoint(q, da, MU1, SG1)) for q, da in zip(planes, steps)]
            finish(planes, g, steps, local, A1, 0, M1, H1)

        def join(p):
            A1[p] = RR[p] + UU[p - 1] + VV[p + 1]

        for dz, dy, part in PIECES_C:
            if dz != 0:
                halo_c[dz, dy, part].start()
        local_c.wait()
        inner(1, forward_one_early)
        wait_for(halo_c, "y")
        for dy in (-1, 1):
            halo_a[0, dy, 0].start()
        inner(1, lambda planes: forward_one(planes, True))
        inner(2, advance)
        inner(3, forward_two)
        local_a.wait()
        wait_for(halo_a, "y")
        for dz, dy, _ in PIECES_A:
            if dz != 0:
                halo_a[dz, dy, 0].start()
        inner(4, back_two(True))
        for p in range(low + 5, high - 4):
            join(p)
        inner(6, back_one_sums)
        wait_for(halo_c, "z")
        outer(1, 6, forward_one)
        outer(2, 5, advance)
        outer(3, 4, forward_two)
        wait_for(halo_a, "z")
        outer(4, 0, back_two(True))
        outer(0, 3, back_two(False))
        for p in [*range(low - 2, low + 5), *range(high - 4, high + 3)]:
            join(p)
        outer(6, 0, back_one_sums)

        both = PACC[pl.ds(0, ROWS)] + PACC[pl.ds(ROWS, ROWS)]
        both = jnp.where(same & (col < 96), both, 0.0)
        gather = (iota((UNITS, ROWS), 1) // 8 == iota((UNITS, ROWS), 0)).astype(F32)
        by_unit = dot(gather, both, HIGH)
        c_row = iota((128, 128), 0)
        c_col = iota((128, 128), 1)
        c_k = jnp.where(c_row < 48, c_row, c_row - 48) // 8
        collect = ((c_k == c_col) & (c_row < 96) & (c_col < 5)).astype(F32)
        grads = dot(by_unit, collect, HIGH) * wo_col
        t_col = jnp.sum(dot(gather, TACC[...], HIGH), axis=1, keepdims=True)
        g_sum = jnp.sum(jnp.sum(GACC[...], axis=0, keepdims=True), axis=1, keepdims=True)
        first_row = iota((UNITS, 128), 0) == 0
        grads = jnp.where(lane == 5, t_col, grads)
        grads = jnp.where((lane == 6) & first_row, g_sum, grads)
        square = jnp.concatenate([grads, jnp.zeros((128 - UNITS, 128), F32)], axis=0)
        by_kind = square.T[0:8]
        kind = iota((8, 128), 0)
        lined = jnp.zeros((8, 128), F32)
        for k in range(4):
            lined = jnp.where((kind & 3) == k, pltpu.roll(by_kind, 32 * k, 1) if k else by_kind, lined)
        MSG[...] = jnp.concatenate([
            jnp.sum(lined[4 * n:4 * n + 4], axis=0, keepdims=True) for n in range(2)], axis=0)

        def exchange(size, ring, place, peer, src, slots, s_sem, r_sem):
            copies = []
            for k in sorted(range(1, size), key=lambda k: abs(k % ring - ring // 2)):
                q, device = peer(k)
                copy = pltpu.make_async_remote_copy(
                    src_ref=src, dst_ref=slots.at[place], send_sem=s_sem.at[k],
                    recv_sem=r_sem.at[place], device_id=device, device_id_type=MESH)
                copy.start()
                copies.append(copy)
            slots[place] = src[...]
            return copies

        def collected(size, peer, copies, src, slots, s_sem, r_sem):
            for k in range(1, size):
                q, device = peer(k)
                pltpu.make_async_remote_copy(
                    src_ref=src, dst_ref=slots.at[q], send_sem=s_sem.at[k],
                    recv_sem=r_sem.at[q], device_id=device, device_id_type=MESH).wait_recv()
            total = slots[0]
            for k in range(1, size):
                total = total + slots[k]
            return total

        sent1 = exchange(size1, n_z, place1, peer1, MSG, RED, rs_send, rs_recv)

        outer(0, 1, back_one_sides)
        inner(4, back_one_rest)
        total = collected(size1, peer1, sent1, MSG, RED, rs_send, rs_recv)
        MSG2[...] = total
        sent2 = exchange(size2, 4, place2, peer2, MSG2, RED2, rs2_send, rs2_recv)
        outer(4, 0, back_one_rest)
        for p in range(low, high + 1):
            rows = pl.ds(R, yl)
            OUTV[p - WC] = RR[p, rows] + UU[p - 1, rows] + VV[p + 1, rows]
        write = pltpu.make_async_copy(OUTV, out, local_sem.at[2])
        write.start()

        total = collected(size2, peer2, sent2, MSG2, RED2, rs2_send, rs2_recv)
        total = total * factor
        spread_rows = jnp.where(kind < 4, total[0:1], total[1:2])
        sums_out = jnp.zeros((8, 128), F32)
        for k in range(4):
            sums_out = jnp.where((kind & 3) == k, pltpu.roll(spread_rows, 128 - 32 * k, 1) if k else spread_rows, sums_out)
        out_sums[...] = sums_out

        for copy in [*halo_c.values(), *halo_a.values(), *sent1, *sent2]:
            copy.wait_send()
        write.wait()

    return kernel, yr, size1, size2


def hand_over(field, sums, out, out_wi, out_bi, out_wo, out_bo):
    out[...] = field[...]
    out_wi[...] = sums[0:4, 0:UNITS]
    out_bi[...] = sums[4:5, 0:UNITS]
    out_wo[...] = sums[5:6, 0:UNITS]
    out_bo[...] = sums[6:7, 0:1]


def per_device(ng, ny, concentration, cotangent, w_in, b_in, w_out, b_out):
    zl, yl, nx = concentration.shape
    factor = 1.0 / (STEP * math.sqrt(float(zl * yl * nx * ng * ny)))
    kernel, yr, size1, size2 = make_kernel(zl, yl, ng, ny, factor)
    planes = zl + 2 * WC
    nv = yl // 8
    field = pltpu.VMEM((planes, yr, nx), F32)
    anywhere = pl.BlockSpec(memory_space=pl.ANY)
    vmem = pl.BlockSpec(memory_space=pltpu.VMEM)
    smem = pl.BlockSpec(memory_space=pltpu.SMEM)
    outs = pl.pallas_call(
        kernel,
        out_shape=(
            jax.ShapeDtypeStruct(concentration.shape, F32),
            jax.ShapeDtypeStruct((8, 128), F32),
        ),
        in_specs=[anywhere, anywhere, vmem, vmem, vmem, smem],
        out_specs=(anywhere, vmem),
        scratch_shapes=[
            field,
            pltpu.VMEM((zl + 2 * WA, yr, nx), F32),
            field, field, field,
            field, field, field, field,
            field, field, field, field,
            pltpu.VMEM((planes, yl + 8, nx), F32),
            pltpu.VMEM((planes, nv + 1, ROWS, nx), F32),
            pltpu.VMEM((planes, nv + 1, ROWS, nx), F32),
            pltpu.VMEM((ROWS, 128), BF16),
            pltpu.VMEM((ROWS, 128), F32),
            pltpu.VMEM((64, ROWS), BF16),
            pltpu.VMEM((2, 2 * ROWS, 2 * yl // 8 * 128), BF16),
            pltpu.VMEM((2 * ROWS, 128), F32),
            pltpu.VMEM((ROWS, 128), F32),
            pltpu.VMEM((8, 128), F32),
            pltpu.VMEM((zl, yl, nx), F32),
            pltpu.VMEM((size1, 2, 128), F32),
            pltpu.VMEM((max(size2, 1), 2, 128), F32),
            pltpu.VMEM((2, 128), F32),
            pltpu.VMEM((2, 128), F32),
            pltpu.SemaphoreType.DMA((2, 12)),
            pltpu.SemaphoreType.DMA((2, 12)),
            pltpu.SemaphoreType.DMA((3,)),
            pltpu.SemaphoreType.DMA((size1,)),
            pltpu.SemaphoreType.DMA((size1,)),
            pltpu.SemaphoreType.DMA((size2,)),
            pltpu.SemaphoreType.DMA((size2,)),
        ],
        compiler_params=pltpu.CompilerParams(
            collective_id=0, has_side_effects=True, vmem_limit_bytes=60 * 1024 * 1024
        ),
    )(
        concentration, cotangent, w_in.T, b_in.reshape(1, UNITS), w_out.reshape(1, UNITS), b_out.reshape(1, 1)
    )
    outs = pl.pallas_call(
        hand_over,
        out_shape=(
            jax.ShapeDtypeStruct(concentration.shape, F32),
            jax.ShapeDtypeStruct((4, UNITS), F32),
            jax.ShapeDtypeStruct((1, UNITS), F32),
            jax.ShapeDtypeStruct((1, UNITS), F32),
            jax.ShapeDtypeStruct((1, 1), F32),
        ),
        in_specs=[vmem, vmem],
        out_specs=(vmem, vmem, vmem, vmem, vmem),
    )(*outs)
    return (outs[0], outs[1].T, outs[2].reshape(UNITS), outs[3].reshape(UNITS), outs[4].reshape(()))


def solution(mesh):
    ng, ny = mesh.shape["gz"], mesh.shape["gy"]
    in_specs = (P("gz", "gy", None), P("gz", "gy", None), P(), P(), P(), P())
    out_specs = (P("gz", "gy", None), P(), P(), P(), P())

    def run(*args):
        return per_device(ng, ny, *args)

    return jax.shard_map(run, mesh=mesh, in_specs=in_specs, out_specs=out_specs, check_vma=False)
```

```python
import math

import jax
import jax.numpy as jnp
from jax import lax
from jax.experimental import pallas as pl
from jax.experimental.pallas import tpu as pltpu
from jax.sharding import PartitionSpec as P

KAPPA = 0.5
STEP = 0.008
FLOOR = 0.05
HIGH = lax.Precision.HIGHEST
MESH = pl.DeviceIdType.MESH
F32 = jnp.float32
BF16 = jnp.bfloat16

WC = 7
WA = 4
R = 8
UNITS = 32
ROWS = UNITS * 8


DIRECTIONS = [(dz, dy) for dz in (0, -1, 1) for dy in (-1, 1, 0) if (dz, dy) != (0, 0)]

CORNER_C = ((0, 2, 8), (2, 4, 4))
CORNER_A = ((0, 3, 4),)
PIECES_C = [(dz, dy, n) for dz, dy in DIRECTIONS for n in range(len(CORNER_C) if dz * dy else 1)]
PIECES_A = [(dz, dy, n) for dz, dy in DIRECTIONS for n in range(len(CORNER_A) if dz * dy else 1)]


def iota(shape, dim):
    return lax.broadcasted_iota(jnp.int32, shape, dim)


def xp(v):
    return pltpu.roll(v, v.shape[1] - 1, 1)


def xm(v):
    return pltpu.roll(v, 1, 1)


def yp(v):
    return pltpu.roll(v, v.shape[0] - 1, 0)


def ym(v):
    return pltpu.roll(v, 1, 0)


def split(v):
    high = v.astype(BF16)
    return high, (v - high.astype(F32)).astype(BF16)


def dot(a, b, precision=None):
    return jnp.dot(a, b, preferred_element_type=F32, precision=precision)


def make_kernel(zl, yl, ng, ny, factor):
    nv = yl // 8
    yr = yl + 2 * R
    n_core = 2 if ny % 2 == 0 else 1
    n_z = 8 if ng % 8 == 0 else 1
    size1 = n_core * n_z
    size2 = (ny // n_core) * (ng // n_z)

    def kernel(
        conc, cot, w_in, b_in, w_out, b_out,
        out, out_sums,
        C, A0, MU1, M1, SG1, C2, MU2, M2, SG2, RR, UU, VV, A1, GS, H1, H2,
        WL, WOF, CT, UB, PACC, TACC, GACC, OUTV, RED, RED2, MSG, MSG2,
        send_sem, recv_sem, local_sem, rs_send, rs_recv, rs2_send, rs2_recv,
    ):
        gz = lax.axis_index("gz")
        gy = lax.axis_index("gy")

        def neighbour(dz, dy):
            return (lax.rem(gz + dz + ng, ng), lax.rem(gy + dy + ny, ny))

        place1 = lax.rem(gy, n_core) * n_z + lax.rem(gz, n_z)
        place2 = (gy // n_core) * (ng // n_z) + gz // n_z

        def peer1(k):
            q = lax.rem(place1 + k, size1)
            return q, (gz // n_z * n_z + lax.rem(q, n_z), gy // n_core * n_core + q // n_z)

        def peer2(k):
            q = lax.rem(place2 + k, size2)
            outer = ng // n_z
            return q, (lax.rem(q, outer) * n_z + lax.rem(gz, n_z), q // outer * n_core + lax.rem(gy, n_core))

        local_c = pltpu.make_async_copy(
            conc, C.at[pl.ds(WC, zl), pl.ds(R, yl)], local_sem.at[0])
        local_a = pltpu.make_async_copy(
            cot, A0.at[pl.ds(WA, zl), pl.ds(R, yl)], local_sem.at[1])
        local_c.start()
        local_a.start()

        barrier = pltpu.get_barrier_semaphore()
        count = 0
        for dz, dy in DIRECTIONS:
            pl.semaphore_signal(barrier, inc=1, device_id=neighbour(dz, dy), device_id_type=MESH)
            count += 1
        for k in range(1, size1):
            pl.semaphore_signal(barrier, inc=1, device_id=peer1(k)[1], device_id_type=MESH)
            count += 1
        for k in range(1, size2):
            pl.semaphore_signal(barrier, inc=1, device_id=peer2(k)[1], device_id_type=MESH)
            count += 1
        pl.semaphore_wait(barrier, count)

        def span(d, size, edge, first, length):
            if d > 0:
                return pl.ds(size - first - length, length), pl.ds(edge - first - length, length)
            if d < 0:
                return pl.ds(first, length), pl.ds(edge + size + first, length)
            return pl.ds(0, size), pl.ds(edge, size)

        def halo(which, source, field, pieces, width, rows, corner):
            copies = {}
            for n, (dz, dy, part) in enumerate(pieces):
                first, planes, high_rows = corner[part] if dz * dy else (0, width, rows)
                sz, tz = span(dz, zl, width, first, planes)
                sy, ty = span(dy, yl, R, 0, high_rows)
                copies[dz, dy, part] = pltpu.make_async_remote_copy(
                    src_ref=source.at[sz, sy],
                    dst_ref=field.at[tz, ty],
                    send_sem=send_sem.at[which, n],
                    recv_sem=recv_sem.at[which, n],
                    device_id=neighbour(dz, dy),
                    device_id_type=MESH,
                )
            return copies

        halo_c = halo(0, conc, C, PIECES_C, WC, 8, CORNER_C)
        halo_a = halo(1, cot, A0, PIECES_A, WA, 4, CORNER_A)
        for dy in (-1, 1):
            halo_c[0, dy, 0].start()

        for margin in (0, R + yl):
            for first, length in ((0, WC - 2), (WC + zl + 2, WC - 2)):
                rows = pl.ds(margin + (0 if margin == 0 else 4), 4)
                C[pl.ds(first, length), rows] = jnp.zeros((length, 4, 128), F32)
            for p in (0, 2 * WC + zl - 1):
                C[p, pl.ds(margin, R)] = jnp.zeros((R, 128), F32)
            rows = pl.ds(margin + (0 if margin == 0 else 4), 4)
            A0[:, rows] = jnp.zeros((zl + 2 * WA, 4, 128), F32)
            for p in (0, 2 * WA + zl - 1):
                A0[p, pl.ds(margin, R)] = jnp.zeros((R, 128), F32)

        lane = iota((UNITS, 128), 1)
        eye = iota((UNITS, UNITS), 0) == iota((UNITS, UNITS), 1)
        bi_col = jnp.sum(jnp.where(eye, b_in[...], 0.0), axis=1, keepdims=True)
        wo_col = jnp.sum(jnp.where(eye, w_out[...], 0.0), axis=1, keepdims=True)
        packed = jnp.where(lane == 4, bi_col, jnp.where(lane == 5, wo_col, 0.0))
        for k in range(4):
            w_col = jnp.sum(jnp.where(eye, w_in[k:k + 1, :], 0.0), axis=1, keepdims=True)
            packed = jnp.where(lane == k, w_col, packed)
        spread = (iota((ROWS, UNITS), 0) // 8 == iota((ROWS, UNITS), 1)).astype(F32)
        params = dot(spread, packed, HIGH)
        row = iota((ROWS, 128), 0)
        col = iota((ROWS, 128), 1)
        same = (row & 7) == (col & 7)
        which_k = (col & 31) // 8
        group = col // 32
        w_sel = jnp.zeros((ROWS, 128), F32)
        for k in range(4):
            w_sel = jnp.where(which_k == k, params[:, k:k + 1], w_sel)
        bias = jnp.broadcast_to(params[:, 4:5], (ROWS, 128))
        wo_full = jnp.broadcast_to(params[:, 5:6], (ROWS, 128))
        WOF[...] = wo_full
        value = jnp.where(group == 3, jnp.where(which_k < 2, bias, 0.0), w_sel)
        high = value.astype(BF16).astype(F32)
        low = value - high
        is_low = (group == 1) | ((group == 3) & (which_k == 1))
        WL[...] = jnp.where(same, jnp.where(is_low, low, high), 0.0).astype(BF16)
        joint = w_sel * wo_full
        j_high = joint.astype(BF16).astype(F32)
        j_low = joint - j_high
        j_mat = jnp.where(same, jnp.where(group == 0, j_high, jnp.where(group == 1, j_low, 0.0)), 0.0)
        CT[...] = j_mat.T[0:64].astype(BF16)
        PACC[...] = jnp.zeros((2 * ROWS, 128), F32)
        TACC[...] = jnp.zeros((ROWS, 128), F32)
        GACC[...] = jnp.zeros((8, 128), F32)

        half = iota((8, 128), 0) < 4

        def pack(v):
            blocks = [v[R + 8 * i:R + 8 * i + 8] for i in range(nv)]
            blocks.append(jnp.where(half, v[R + yl:], v[:R]))
            return blocks

        def unpack(blocks):
            return jnp.concatenate([blocks[-1]] + blocks[:-1] + [blocks[-1]], axis=0)

        def fields_of(c_ref, p, rows=slice(None)):
            c = c_ref[p, rows]
            zu, zd = c_ref[p + 1, rows], c_ref[p - 1, rows]
            yu, yd = yp(c), ym(c)
            xu, xd = xp(c), xm(c)
            lap = ((zu + zd) + (yu + yd)) + (xu + xd) - 6.0 * c
            s0, s1, s2 = 0.5 * (zu - zd), 0.5 * (yu - yd), 0.5 * (xu - xd)
            sq = s0 * s0 + s1 * s1 + s2 * s2
            return c, lap, sq, (s0, s1, s2)

        def units(pair):
            feats = jnp.concatenate([jnp.concatenate(f, axis=0) for f in pair], axis=1)
            f_high, f_low = split(feats)
            rhs = jnp.concatenate([f_high, f_high, f_low, jnp.ones((32, 256), BF16)], axis=0)
            return jnp.tanh(dot(WL[...], rhs))

        def score(h):
            wo = WOF[...]
            weighted = h * jnp.concatenate([wo, wo], axis=1)
            return jnp.sum(weighted.reshape(UNITS, 8, 256), axis=0) + b_out[0, 0]

        def soft(s):
            e = jnp.exp(s)
            return jnp.log(1.0 + e) + FLOOR, e / (1.0 + e)

        def forward_blocks(q, feats, ids, offset):
            pair = [[f[8 * i - offset:8 * i - offset + 8] for f in feats] for i in ids]
            h = units(pair)
            if ids[0] > nv:
                mask = (iota((ROWS, 128), 0) & 7) < 4
                H1[q, nv] = jnp.where(mask, h[:, :128], h[:, 128:])
            else:
                for i in range(2):
                    H1[q, ids[i] - 1] = h[:, 128 * i:128 * i + 128]
            m, sg = soft(score(h))
            for i in range(2):
                rows = pl.ds(8 * ids[i], 8)
                M1[q, rows] = m[:, 128 * i:128 * i + 128]
                SG1[q, rows] = sg[:, 128 * i:128 * i + 128]

        def forward_one_early(planes):
            for q in planes:
                c, lap, sq, _ = fields_of(C, q, pl.ds(R, yl))
                feats = [c, lap, sq, c * c * c - c - KAPPA * lap]
                for i in range(2, nv, 2):
                    forward_blocks(q, feats, (i, i + 1), R)

        def forward_one(planes, early=False, sides=True):
            for q in planes:
                c, lap, sq, _ = fields_of(C, q)
                mu = c * c * c - c - KAPPA * lap
                MU1[q] = mu
                feats = [c, lap, sq, mu]
                if not early:
                    for i in range(2, nv, 2):
                        forward_blocks(q, feats, (i, i + 1), 0)
                forward_blocks(q, feats, (1, nv), 0)
                if sides:
                    forward_blocks(q, feats, (nv + 1, 0), 0)
                else:
                    for i in (0, nv + 1):
                        M1[q, pl.ds(8 * i, 8)] = jnp.zeros((8, 128), F32)

        def wait_for(copies, sides):
            for dz, dy, part in copies:
                if (dz == 0) == (sides == "y"):
                    copies[dz, dy, part].wait_recv()

        low, high = WC, WC + zl - 1

        def inner(width, body):
            for p in range(low + width, high - width, 2):
                body((p, p + 1))

        def outer(first, last, body):
            for k in range(-first, last):
                body((low - 1 - k, high + 1 + k))

        def advance(planes):
            for p in planes:
                advance_plane(p)

        def advance_plane(p):
            mu, m = MU1[p], M1[p]
            def face(mu_a, m_a, mu_b, m_b):
                return (m_a + m_b) * (mu_b - mu_a)
            up = face(mu, m, MU1[p + 1], M1[p + 1])
            down = face(MU1[p - 1], M1[p - 1], mu, m)
            fy = face(mu, m, yp(mu), yp(m))
            fx = face(mu, m, xp(mu), xp(m))
            total = (up - down) + (fy - ym(fy)) + (fx - xm(fx))
            C2[p] = C[p] + (0.5 * STEP) * total

        def forward_two(planes):
            feats = []
            for q in planes:
                c, lap, sq, _ = fields_of(C2, q)
                mu = c * c * c - c - KAPPA * lap
                MU2[q] = mu
                feats.append([pack(f) for f in (c, lap, sq, mu)])
            work = [((d, a), (d, a + 1)) for d in range(2) for a in range(0, nv, 2)] + [((0, nv), (1, nv))]
            for places in work:
                h = units([[f[a] for f in feats[d]] for d, a in places])
                m, sg = soft(score(h))
                for i, (d, a) in enumerate(places):
                    q = planes[d]
                    H2[q, a] = h[:, 128 * i:128 * i + 128]
                    mi, si = m[:, 128 * i:128 * i + 128], sg[:, 128 * i:128 * i + 128]
                    for start in ([R + 8 * a] if a < nv else [0, R + yl]):
                        M2[q, pl.ds(start, 8)] = mi
                        SG2[q, pl.ds(start, 8)] = si

        def jumps(q, adj, shift):
            a = adj[q + shift]
            return adj[q + 1 + shift] - a, a - adj[q - 1 + shift], yp(a) - a, xp(a) - a

        def faces(field, q, da, of):
            v = field[q]
            up = of(v, field[q + 1], da[0])
            down = of(field[q - 1], v, da[1])
            fy = of(v, yp(v), da[2])
            fx = of(v, xp(v), da[3])
            return (up, down), (fy, ym(fy)), (fx, xm(fx))

        def score_adjoint(q, da, mu_ref, sg_ref):
            z, y, x = faces(mu_ref, q, da, lambda here, there, d: (there - here) * d)
            adj_mob = (z[0] + z[1]) + (y[0] + y[1]) + (x[0] + x[1])
            return (-0.5 * STEP) * adj_mob * sg_ref[q]

        def flux_adjoint(q, da, m_ref):
            z, y, x = faces(m_ref, q, da, lambda here, there, d: (here + there) * d)
            return (0.5 * STEP) * ((z[0] - z[1]) + (y[0] - y[1]) + (x[0] - x[1]))

        def places_of(with_core, with_sides):
            core = [((d, b), (d, b + 1)) for d in range(2) for b in range(0, nv, 2)] if with_core else []
            return core + ([((0, nv), (1, nv))] if with_sides else [])

        def hidden(planes, places, h_ref):
            h = jnp.concatenate([h_ref[planes[d], b] for d, b in places], axis=1)
            return 1.0 - h * h

        def sums(planes, g, local, mu_ref, h_ref, ub):
            feats = []
            for q, (c, lap, sq, _) in zip(planes, local):
                feats.append([pack(f) for f in (c, lap, sq, mu_ref[q])])
            gg = []
            for n, places in enumerate(places_of(True, False)):
                u = hidden(planes, places, h_ref)
                u_high, u_low = split(u)
                ub[pl.ds(0, ROWS), pl.ds(256 * n, 256)] = u_high
                ub[pl.ds(ROWS, ROWS), pl.ds(256 * n, 256)] = u_low
                gs = jnp.concatenate([g[d][b] for d, b in places], axis=1)
                stack = [gs * jnp.concatenate([feats[d][k][b] for d, b in places], axis=1) for k in range(4)]
                s_high, s_low = split(jnp.concatenate(stack + [gs, jnp.zeros((8, 256), F32)], axis=0))
                gg.append(jnp.concatenate([s_high, s_low, jnp.zeros((32, 256), BF16)], axis=0))
            PACC[...] += lax.dot_general(
                ub[...], jnp.concatenate(gg, axis=1), (((1,), (1,)), ((), ())), preferred_element_type=F32)
            total = TACC[...].reshape(UNITS, 8, 128)
            g_total = GACC[...]
            for d in range(2):
                for b in range(nv):
                    total = total + h_ref[planes[d], b].reshape(UNITS, 8, 128) * g[d][b][None]
                    g_total = g_total + g[d][b]
            TACC[...] = total.reshape(ROWS, 128)
            GACC[...] = g_total

        def finish(planes, g, steps, local, adj, shift, m_ref, h_ref, ub=None):
            A = [[None] * (nv + 1) for _ in planes]
            for n, places in enumerate(places_of(True, True)):
                if ub is not None and n < nv:
                    u_high = ub[pl.ds(0, ROWS), pl.ds(256 * n, 256)]
                else:
                    u_high = hidden(planes, places, h_ref).astype(BF16)
                back = dot(CT[...], u_high)
                back = back[:32] + back[32:]
                for i, (d, b) in enumerate(places):
                    A[d][b] = [back[8 * k:8 * k + 8, 128 * i:128 * i + 128] * g[d][b] for k in range(4)]
            for d, q in enumerate(planes):
                a_c, a_lap, a_sq, a_mu = (unpack([A[d][b][k] for b in range(nv + 1)]) for k in range(4))
                c, _, _, slopes = local[d]
                adj_pot = flux_adjoint(q, steps[d], m_ref) + a_mu
                adj_lap = a_lap - KAPPA * adj_pot
                zed, why, ex = (a_sq * slope for slope in slopes)
                rest = adj[q + shift] + a_c + (3.0 * c * c - 1.0) * adj_pot - 6.0 * adj_lap
                rest = rest + (xm(adj_lap + ex) + xp(adj_lap - ex)) + (ym(adj_lap + why) + yp(adj_lap - why))
                RR[q] = rest
                UU[q] = adj_lap + zed
                VV[q] = adj_lap - zed

        turn = [0]

        def buffer():
            turn[0] ^= 1
            return UB.at[turn[0]]

        def start_of(planes, adj, shift, c_ref):
            return [jumps(q, adj, shift) for q in planes], [fields_of(c_ref, q) for q in planes]

        def back_two(with_sums):
            def body(planes):
                shift = WA - WC
                steps, local = start_of(planes, A0, shift, C2)
                g = [pack(score_adjoint(q, da, MU2, SG2)) for q, da in zip(planes, steps)]
                ub = buffer() if with_sums else None
                if with_sums:
                    sums(planes, g, local, MU2, H2, ub)
                finish(planes, g, steps, local, A0, shift, M2, H2, ub)
            return body

        def back_one_sums(planes):
            steps, local = start_of(planes, A1, 0, C)
            g = [pack(score_adjoint(q, da, MU1, SG1)) for q, da in zip(planes, steps)]
            sums(planes, g, local, MU1, H1, buffer())
            for d, q in enumerate(planes):
                for b in range(nv + 1):
                    GS[q, pl.ds(8 * b, 8)] = g[d][b]

        def back_one_rest(planes):
            steps, local = start_of(planes, A1, 0, C)
            g = [[GS[q, pl.ds(8 * b, 8)] for b in range(nv + 1)] for q in planes]
            finish(planes, g, steps, local, A1, 0, M1, H1)

        def back_one_sides(planes):
            steps, local = start_of(planes, A1, 0, C)
            g = [pack(score_adjoint(q, da, MU1, SG1)) for q, da in zip(planes, steps)]
            finish(planes, g, steps, local, A1, 0, M1, H1)

        def join(p):
            A1[p] = RR[p] + UU[p - 1] + VV[p + 1]

        for dz, dy, part in PIECES_C:
            if dz != 0:
                halo_c[dz, dy, part].start()
        local_c.wait()
        inner(1, forward_one_early)
        wait_for(halo_c, "y")
        for dy in (-1, 1):
            halo_a[0, dy, 0].start()
        inner(1, lambda planes: forward_one(planes, True))
        inner(2, advance)
        inner(3, forward_two)
        local_a.wait()
        wait_for(halo_a, "y")
        for dz, dy, _ in PIECES_A:
            if dz != 0:
                halo_a[dz, dy, 0].start()
        inner(4, back_two(True))
        for p in range(low + 5, high - 4):
            join(p)
        inner(6, back_one_sums)
        wait_for(halo_c, "z")
        outer(1, 5, forward_one)
        forward_one((low - 6, high + 6), sides=False)
        outer(2, 5, advance)
        outer(3, 4, forward_two)
        wait_for(halo_a, "z")
        outer(4, 0, back_two(True))
        outer(0, 3, back_two(False))
        for p in [*range(low - 2, low + 5), *range(high - 4, high + 3)]:
            join(p)
        outer(6, 0, back_one_sums)

        both = PACC[pl.ds(0, ROWS)] + PACC[pl.ds(ROWS, ROWS)]
        both = jnp.where(same & (col < 96), both, 0.0)
        gather = (iota((UNITS, ROWS), 1) // 8 == iota((UNITS, ROWS), 0)).astype(F32)
        by_unit = dot(gather, both, HIGH)
        c_row = iota((128, 128), 0)
        c_col = iota((128, 128), 1)
        c_k = jnp.where(c_row < 48, c_row, c_row - 48) // 8
        collect = ((c_k == c_col) & (c_row < 96) & (c_col < 5)).astype(F32)
        grads = dot(by_unit, collect, HIGH) * wo_col
        t_col = jnp.sum(dot(gather, TACC[...], HIGH), axis=1, keepdims=True)
        g_sum = jnp.sum(jnp.sum(GACC[...], axis=0, keepdims=True), axis=1, keepdims=True)
        first_row = iota((UNITS, 128), 0) == 0
        grads = jnp.where(lane == 5, t_col, grads)
        grads = jnp.where((lane == 6) & first_row, g_sum, grads)
        square = jnp.concatenate([grads, jnp.zeros((128 - UNITS, 128), F32)], axis=0)
        by_kind = square.T[0:8]
        kind = iota((8, 128), 0)
        lined = jnp.zeros((8, 128), F32)
        for k in range(4):
            lined = jnp.where((kind & 3) == k, pltpu.roll(by_kind, 32 * k, 1) if k else by_kind, lined)
        MSG[...] = jnp.concatenate([
            jnp.sum(lined[4 * n:4 * n + 4], axis=0, keepdims=True) for n in range(2)], axis=0)

        def exchange(size, ring, place, peer, src, slots, s_sem, r_sem):
            copies = []
            for k in sorted(range(1, size), key=lambda k: abs(k % ring - ring // 2)):
                q, device = peer(k)
                copy = pltpu.make_async_remote_copy(
                    src_ref=src, dst_ref=slots.at[place], send_sem=s_sem.at[k],
                    recv_sem=r_sem.at[place], device_id=device, device_id_type=MESH)
                copy.start()
                copies.append(copy)
            slots[place] = src[...]
            return copies

        def collected(size, peer, copies, src, slots, s_sem, r_sem):
            for k in range(1, size):
                q, device = peer(k)
                pltpu.make_async_remote_copy(
                    src_ref=src, dst_ref=slots.at[q], send_sem=s_sem.at[k],
                    recv_sem=r_sem.at[q], device_id=device, device_id_type=MESH).wait_recv()
            total = slots[0]
            for k in range(1, size):
                total = total + slots[k]
            return total

        sent1 = exchange(size1, n_z, place1, peer1, MSG, RED, rs_send, rs_recv)

        outer(0, 1, back_one_sides)
        inner(4, back_one_rest)
        total = collected(size1, peer1, sent1, MSG, RED, rs_send, rs_recv)
        MSG2[...] = total
        sent2 = exchange(size2, 4, place2, peer2, MSG2, RED2, rs2_send, rs2_recv)
        outer(4, 0, back_one_rest)
        for p in range(low, high + 1):
            rows = pl.ds(R, yl)
            OUTV[p - WC] = RR[p, rows] + UU[p - 1, rows] + VV[p + 1, rows]
        write = pltpu.make_async_copy(OUTV, out, local_sem.at[2])
        write.start()

        total = collected(size2, peer2, sent2, MSG2, RED2, rs2_send, rs2_recv)
        total = total * factor
        spread_rows = jnp.where(kind < 4, total[0:1], total[1:2])
        sums_out = jnp.zeros((8, 128), F32)
        for k in range(4):
            sums_out = jnp.where((kind & 3) == k, pltpu.roll(spread_rows, 128 - 32 * k, 1) if k else spread_rows, sums_out)
        out_sums[...] = sums_out

        for copy in [*halo_c.values(), *halo_a.values(), *sent1, *sent2]:
            copy.wait_send()
        write.wait()

    return kernel, yr, size1, size2


def hand_over(field, sums, out, out_wi, out_bi, out_wo, out_bo):
    out[...] = field[...]
    out_wi[...] = sums[0:4, 0:UNITS]
    out_bi[...] = sums[4:5, 0:UNITS]
    out_wo[...] = sums[5:6, 0:UNITS]
    out_bo[...] = sums[6:7, 0:1]


def per_device(ng, ny, concentration, cotangent, w_in, b_in, w_out, b_out):
    zl, yl, nx = concentration.shape
    factor = 1.0 / (STEP * math.sqrt(float(zl * yl * nx * ng * ny)))
    kernel, yr, size1, size2 = make_kernel(zl, yl, ng, ny, factor)
    planes = zl + 2 * WC
    nv = yl // 8
    field = pltpu.VMEM((planes, yr, nx), F32)
    anywhere = pl.BlockSpec(memory_space=pl.ANY)
    vmem = pl.BlockSpec(memory_space=pltpu.VMEM)
    smem = pl.BlockSpec(memory_space=pltpu.SMEM)
    outs = pl.pallas_call(
        kernel,
        out_shape=(
            jax.ShapeDtypeStruct(concentration.shape, F32),
            jax.ShapeDtypeStruct((8, 128), F32),
        ),
        in_specs=[anywhere, anywhere, vmem, vmem, vmem, smem],
        out_specs=(anywhere, vmem),
        scratch_shapes=[
            field,
            pltpu.VMEM((zl + 2 * WA, yr, nx), F32),
            field, field, field,
            field, field, field, field,
            field, field, field, field,
            pltpu.VMEM((planes, yl + 8, nx), F32),
            pltpu.VMEM((planes, nv + 1, ROWS, nx), F32),
            pltpu.VMEM((planes, nv + 1, ROWS, nx), F32),
            pltpu.VMEM((ROWS, 128), BF16),
            pltpu.VMEM((ROWS, 128), F32),
            pltpu.VMEM((64, ROWS), BF16),
            pltpu.VMEM((2, 2 * ROWS, 2 * yl // 8 * 128), BF16),
            pltpu.VMEM((2 * ROWS, 128), F32),
            pltpu.VMEM((ROWS, 128), F32),
            pltpu.VMEM((8, 128), F32),
            pltpu.VMEM((zl, yl, nx), F32),
            pltpu.VMEM((size1, 2, 128), F32),
            pltpu.VMEM((max(size2, 1), 2, 128), F32),
            pltpu.VMEM((2, 128), F32),
            pltpu.VMEM((2, 128), F32),
            pltpu.SemaphoreType.DMA((2, 12)),
            pltpu.SemaphoreType.DMA((2, 12)),
            pltpu.SemaphoreType.DMA((3,)),
            pltpu.SemaphoreType.DMA((size1,)),
            pltpu.SemaphoreType.DMA((size1,)),
            pltpu.SemaphoreType.DMA((size2,)),
            pltpu.SemaphoreType.DMA((size2,)),
        ],
        compiler_params=pltpu.CompilerParams(
            collective_id=0, has_side_effects=True, vmem_limit_bytes=60 * 1024 * 1024
        ),
    )(
        concentration, cotangent, w_in.T, b_in.reshape(1, UNITS), w_out.reshape(1, UNITS), b_out.reshape(1, 1)
    )
    outs = pl.pallas_call(
        hand_over,
        out_shape=(
            jax.ShapeDtypeStruct(concentration.shape, F32),
            jax.ShapeDtypeStruct((4, UNITS), F32),
            jax.ShapeDtypeStruct((1, UNITS), F32),
            jax.ShapeDtypeStruct((1, UNITS), F32),
            jax.ShapeDtypeStruct((1, 1), F32),
        ),
        in_specs=[vmem, vmem],
        out_specs=(vmem, vmem, vmem, vmem, vmem),
    )(*outs)
    return (outs[0], outs[1].T, outs[2].reshape(UNITS), outs[3].reshape(UNITS), outs[4].reshape(()))


def solution(mesh):
    ng, ny = mesh.shape["gz"], mesh.shape["gy"]
    in_specs = (P("gz", "gy", None), P("gz", "gy", None), P(), P(), P(), P())
    out_specs = (P("gz", "gy", None), P(), P(), P(), P())

    def run(*args):
        return per_device(ng, ny, *args)

    return jax.shard_map(run, mesh=mesh, in_specs=in_specs, out_specs=out_specs, check_vma=False)
```
